128 devices in a mesh: lat: 32 (over y, z, core), fld: 4 (over x).
Axes of the slice: x: 4, y: 4, z: 4, core: 2. Of those that a mesh axis runs over, the one named last changes fastest.
Arguments:
- grid: bfloat16 [20, 32, 2, 5248], P('fld', 'lat'), may hold values from -6 to 6
- row_lengths: int32 [32], replicated, may hold values from 20 to 5136, as said below
- band_map: int32 [32], replicated, may hold values from 0 to 31, each once
- fold_map: int32 [128, 10], replicated, may hold values from 0 to 1279, as said below
- legendre: float32 [640, 1281, 32], P(('lat', 'fld')), may hold values from -0.75 to 0.75
- to_modes: float32 [20, 20], replicated, may hold values from -1.25 to 1.25
- back_modes: float32 [20, 20], replicated, may hold values from -1.25 to 1.25
- mode_rates: float32 [20], replicated, may hold values from 0.1 to 30
Outputs:
- spectral: float32 [20, 2, 640, 1281], P(None, None, ('lat', 'fld'))
- grid_out: bfloat16 [20, 32, 2, 5248], P('fld', 'lat')
The draws below stay inside these ranges and needn't reach their ends.
Inputs may be any that keep to these rules, and one draw needn't show every extreme that they name: `row_lengths`: entry j is 20 + 4 i for an octahedral row index i with j * S <= i < (j + 1) * S, S = 40; entry 0 is 20 and the last entry is 5136; every entry is a multiple of 4. `fold_map`: every wavenumber 0 to 1279 stands exactly once; in every row, entries 2 s and 2 s + 1 are m and 1279 - m with m < 640. Row d lists the wavenumbers of the device with joined index d of lat+fld (lat index times the size of fld plus fld index). `band_map`: A permutation.
All inputs are finite; a program needn't handle non-finite values.
Results may differ from the reference program's by a relative error of at most 0.006.
Values sent between devices are 32-bit elements; how exact they have to be, the bound alone decides.
A program may use at most 64 MiB of HBM per device.

```python
import math
import jax
import jax.numpy as jnp
from jax import lax

TRUNC = 1279
FL = 20
NSP = 1281
NPAIRS = 640
MDEV = 10
BANDS = 32
NLATH = 32
ROWS = 2
GRIDW = 5248
N_LAT = 32


def draw_row_lengths(key, part):
    key = jax.random.fold_in(key, 11)
    stride = (TRUNC + 1) // NLATH
    base = jnp.arange(NLATH, dtype=jnp.int32) * stride
    step = jax.random.randint(key, (NLATH,), 0, stride, dtype=jnp.int32)
    index = base + step
    index = index.at[0].set(0).at[NLATH - 1].set(TRUNC)
    return (20 + 4 * index).astype(jnp.int32)


def draw_fold_map(key, part):
    key = jax.random.fold_in(key, 23)
    order = jax.random.permutation(key, NPAIRS).astype(jnp.int32)
    paired = jnp.stack([order, TRUNC - order], axis=1)
    return paired.reshape(-1, MDEV).astype(jnp.int32)


def block_levels(own_key, dims, split, least, top_value):
    gain, own = 1.0, jax.random.fold_in(own_key, 6)
    for dim, blocks in split:
        steps = jnp.exp(jax.random.uniform(jax.random.fold_in(own, dim), (blocks,), jnp.float32, least / len(split), top_value / len(split)))
        gain = gain * jnp.repeat(steps, dims[dim] // blocks).reshape([-1 if axis == dim else 1 for axis in range(len(dims))])
    return gain


def noise(key, dims, deviation, reach, cuts=(), held_as=jnp.bfloat16):
    level = block_levels(key, dims, cuts, -0.22, 0.18) if cuts else 1.0
    drawn = jax.random.normal(key, dims, jnp.float32) * deviation * level
    return jnp.minimum(jnp.maximum(drawn, -reach), reach).astype(held_as)


def setup_inputs(seed: int = 0) -> dict:
    streams_of = jax.random.split(jax.random.key(seed), 9)
    return {
        "grid": noise(streams_of[0], (FL, BANDS, ROWS, GRIDW), 1.0, 6.0, ((0, 4), (1, 32))),
        "row_lengths": draw_row_lengths(jax.random.fold_in(streams_of[8], 71), 0),
        "band_map": jax.random.permutation(streams_of[2], N_LAT).astype(jnp.int32),
        "fold_map": draw_fold_map(jax.random.fold_in(streams_of[8], 71), 0),
        "legendre": noise(streams_of[4], (NPAIRS, NSP, NLATH), (2 * NLATH) ** -0.5, 0.75, ((0, 128),), jnp.float32),
        "to_modes": noise(streams_of[5], (FL, FL), FL ** -0.5, 1.25, (), jnp.float32),
        "back_modes": noise(streams_of[6], (FL, FL), FL ** -0.5, 1.25, (), jnp.float32),
        "mode_rates": jnp.clip(jnp.exp(jax.random.uniform(streams_of[7], (FL,), jnp.float32, math.log(0.1), math.log(30.0))), 0.1, 30.0),
    }


HIGH = lax.Precision.HIGHEST
TWO_PI = 2.0 * math.pi

def row_tables(length, quarter_pad, cut_off):
    quarter = length // 4
    top = jnp.minimum(cut_off, (length - 1) // 2)
    across = jnp.arange(quarter_pad, dtype=jnp.int32)[:, None]
    wave = jnp.arange(cut_off + 1, dtype=jnp.int32)[None, :]
    keep = (across < quarter) & (wave <= top)
    inner = (across * wave % quarter).astype(jnp.float32) * (TWO_PI / quarter.astype(jnp.float32))
    cos_table = jnp.where(keep, jnp.cos(inner), 0.0).astype(jnp.bfloat16)
    sin_table = jnp.where(keep, jnp.sin(inner), 0.0).astype(jnp.bfloat16)
    phase = jnp.arange(4, dtype=jnp.int32)[:, None]
    twist = (phase * wave % length).astype(jnp.float32) * (TWO_PI / length.astype(jnp.float32))
    weight = jnp.where(wave == 0, 1.0, 2.0) * (wave <= top).astype(jnp.float32)
    scale = 1.0 / jnp.sqrt(length.astype(jnp.float32))
    return (cos_table, sin_table, jnp.cos(twist), jnp.sin(twist), weight, scale)

def forward_row(values, length, cut_off):
    cos_table, sin_table, cos_twist, sin_twist, weight, scale = row_tables(length, values.shape[1], cut_off)
    wide = values.astype(jnp.float32)
    real_part = jnp.einsum('fab,am->bfm', wide, cos_table.astype(jnp.float32), precision=HIGH)
    imag_part = -jnp.einsum('fab,am->bfm', wide, sin_table.astype(jnp.float32), precision=HIGH)
    cos_b = cos_twist[:, None, :]
    sin_b = sin_twist[:, None, :]
    four_re = scale * lax.optimization_barrier(jnp.sum(cos_b * real_part + sin_b * imag_part, axis=0))
    four_im = scale * lax.optimization_barrier(jnp.sum(cos_b * imag_part - sin_b * real_part, axis=0))
    return jnp.stack([four_re, four_im], axis=1)

def inverse_row(four, length, quarter_pad, cut_off):
    cos_table, sin_table, cos_twist, sin_twist, weight, scale = row_tables(length, quarter_pad, cut_off)
    fields = four.shape[0]
    cos_b = cos_twist[:, None, :]
    sin_b = sin_twist[:, None, :]
    four_re = (four[:, 0] * weight)[None]
    four_im = (four[:, 1] * weight)[None]
    twisted_re = (cos_b * four_re - sin_b * four_im).astype(jnp.bfloat16)
    twisted_im = (sin_b * four_re + cos_b * four_im).astype(jnp.bfloat16)
    total = jnp.einsum('bfm,am->fab', twisted_re.astype(jnp.float32), cos_table.astype(jnp.float32), precision=HIGH)
    total = total - jnp.einsum('bfm,am->fab', twisted_im.astype(jnp.float32), sin_table.astype(jnp.float32), precision=HIGH)
    return (scale * total).reshape(fields, quarter_pad * 4).astype(jnp.bfloat16)

def pair_layout(first, cut_off):
    place = jnp.arange(cut_off + 2, dtype=jnp.int32)[None, :]
    start = first[:, None]
    second = cut_off - start
    partner = place > second
    degree = jnp.where(partner, place - 1, start + place)
    wave = jnp.where(partner, second, start)
    odd = (degree + wave) % 2 == 1
    return (partner, odd, degree)

def direct_legendre(sym, asym, table, partner, odd):
    nlat, fields, two, slots = sym.shape
    pairs = slots // 2
    both = jnp.stack([sym, asym], axis=1).reshape(nlat, 2, fields, 2, pairs, 2)
    stacked = jnp.transpose(both, (4, 0, 5, 1, 2, 3)).reshape(pairs, nlat, 8 * fields)
    raw = jnp.einsum('pqj,pjx->pqx', table, stacked, precision=HIGH)
    raw = raw.reshape(pairs, table.shape[1], 2, 2, fields, 2)
    pick = jnp.where(partner[:, :, None, None, None], raw[:, :, 1], raw[:, :, 0])
    pick = jnp.where(odd[:, :, None, None], pick[:, :, 1], pick[:, :, 0])
    return jnp.transpose(pick, (2, 3, 0, 1))

def inverse_legendre(spectral, table, partner, odd):
    fields = spectral.shape[0]
    pairs, places, nlat = table.shape
    coef = jnp.transpose(spectral, (2, 3, 0, 1))
    parts = []
    for chosen in (jnp.logical_not(partner), partner):
        for parity in (jnp.logical_not(odd), odd):
            parts.append(jnp.where((chosen & parity)[:, :, None, None], coef, 0.0))
    spread = jnp.stack(parts, axis=2).reshape(pairs, places, 8 * fields)
    sums = jnp.einsum('pqj,pqx->pjx', table, spread, precision=HIGH).reshape(pairs, nlat, 2, 2, fields, 2)
    north = sums[:, :, :, 0] + sums[:, :, :, 1]
    south = sums[:, :, :, 0] - sums[:, :, :, 1]
    north = jnp.transpose(north, (1, 3, 4, 0, 2)).reshape(nlat, fields, 2, 2 * pairs)
    south = jnp.transpose(south, (1, 3, 4, 0, 2)).reshape(nlat, fields, 2, 2 * pairs)
    return (north, south)

def implicit_solve(raw, degree, cut_off, to_modes, back_modes, mode_rates):
    modes = jnp.einsum('kf,fcpq->kcpq', to_modes, raw, precision=HIGH)
    tau = (degree * (degree + 1)).astype(jnp.float32) / float(cut_off * (cut_off + 1))
    damped = modes / (1.0 + tau[None, None] * mode_rates[:, None, None, None])
    return jnp.einsum('gk,kcpq->gcpq', back_modes, damped, precision=HIGH)

def reference(grid, row_lengths, band_map, fold_map, legendre, to_modes, back_modes, mode_rates):
    fields, bands, rows, width = grid.shape
    lat_dev = rows // 2
    quarter_pad = width // 4
    pairs_all, places, nlat = legendre.shape
    cut_off = places - 2
    band_rows = band_map[:, None] * lat_dev + jnp.arange(rows, dtype=jnp.int32)[None, :] % lat_dev
    lengths = row_lengths[band_rows].reshape(-1)
    values = jnp.transpose(grid.reshape(fields, bands * rows, quarter_pad, 4), (1, 0, 2, 3))
    four = lax.map(lambda item: forward_row(item[0], item[1], cut_off), (values, lengths))
    by_band = four.reshape(bands, rows, fields, 2, cut_off + 1)[jnp.argsort(band_map)]
    north = by_band[:, :lat_dev].reshape(nlat, fields, 2, cut_off + 1)
    south = by_band[:, lat_dev:].reshape(nlat, fields, 2, cut_off + 1)
    order = fold_map.reshape(-1)
    sym = (north + south)[..., order]
    asym = (north - south)[..., order]
    partner, odd, degree = pair_layout(order[0::2], cut_off)
    raw = direct_legendre(sym, asym, legendre, partner, odd)
    spectral = implicit_solve(raw, degree, cut_off, to_modes, back_modes, mode_rates)
    north_back, south_back = inverse_legendre(spectral, legendre, partner, odd)
    empty = jnp.zeros((nlat, fields, 2, cut_off + 1), jnp.float32)
    north_back = empty.at[..., order].set(north_back)
    south_back = empty.at[..., order].set(south_back)
    rows_back = jnp.concatenate([north_back.reshape(bands, lat_dev, fields, 2, cut_off + 1), south_back.reshape(bands, lat_dev, fields, 2, cut_off + 1)], axis=1)[band_map]
    outgoing = lax.map(lambda item: inverse_row(item[0], item[1], quarter_pad, cut_off), (rows_back.reshape(bands * rows, fields, 2, cut_off + 1), lengths))
    grid_out = jnp.transpose(outgoing.reshape(bands, rows, fields, width), (2, 0, 1, 3))
    return (spectral, grid_out)
```

```python
import functools
import math

import jax
import jax.numpy as jnp
from jax import lax
from jax.experimental import pallas as pl
from jax.experimental.pallas import tpu as pltpu
from jax.sharding import PartitionSpec as P

HIGH = lax.Precision.HIGHEST
MESH = pl.DeviceIdType.MESH
F32, BF16, I32 = jnp.float32, jnp.bfloat16, jnp.int32
NT = (((1,), (1,)), ((), ()))

LAT, FLD = 32, 4
DEVS = LAT * FLD
FIELDS = 5
ALL_FIELDS = FIELDS * FLD
SLOTS = 10
PAIRS = SLOTS // 2
PLACES = 1281
CUT = 1279
WIDTH = 5248
WAVES = DEVS * SLOTS
ACROSS = 1296
STEP = 16
BLOCKS = ACROSS // STEP
LANES = 1408
CHUNK = 512
CHUNKS = 11


def iota(shape, dim):
    return lax.broadcasted_iota(I32, shape, dim)


def dot(a, b, precision=None):
    return jnp.dot(a, b, precision=precision, preferred_element_type=F32)


def dot_nt(a, b):
    return lax.dot_general(a, b, NT, preferred_element_type=F32)


SIN_TERMS = [(-1) ** k * math.pi ** (2 * k + 1) / math.factorial(2 * k + 1) for k in range(6)]
COS_TERMS = [(-1) ** k * math.pi ** (2 * k) / math.factorial(2 * k) for k in range(7)]


def horner(terms, square):
    total = jnp.full_like(square, terms[-1])
    for term in terms[-2::-1]:
        total = total * square + term
    return total


def turn(product, period, inverse):
    rest = product - period * jnp.round(product * inverse)
    part = rest * inverse
    square = part * part
    half_sin = part * horner(SIN_TERMS, square)
    half_cos = horner(COS_TERMS, square)
    return 1.0 - 2.0 * half_sin * half_sin, 2.0 * half_sin * half_cos


def split(value):
    upper = value.astype(BF16)
    return upper, (value - upper.astype(F32)).astype(BF16)


def row_of(value):
    return jnp.concatenate([value[s : s + 1] for s in range(SLOTS)], axis=1)


def kernel(
    len_ref, band_s_ref, fold_s_ref, fold_ref, band_ref, grid_ref, leg_ref, to_ref, back_ref, rate_ref,
    spec_ref, out_ref,
    cos_tab, sin_tab, wc_ref, ws_ref, sel_ref, leg4_ref, inv_ref, acc_c, acc_s, zc_ref, zs_ref, mat_ref, perm_ref, turned,
    send1, recv1, send2, recv2, sems,
):
    lat = lax.axis_index("lat")
    fld = lax.axis_index("fld")
    owner = lat * FLD + fld

    barrier = pltpu.get_barrier_semaphore()

    def greet(k, carry):
        other = lax.rem(owner + k, DEVS)
        pl.semaphore_signal(
            barrier, inc=1, device_id={"lat": other // FLD, "fld": lax.rem(other, FLD)}, device_id_type=MESH
        )
        return carry

    lax.fori_loop(1, DEVS, greet, 0)

    length = len_ref[band_s_ref[lat]]
    waves = row_of(fold_ref[...].astype(F32))
    full = jnp.full((1, WAVES), length.astype(F32), F32)
    quarter = full * 0.25
    inv_quarter = 1.0 / quarter
    scale = 1.0 / jnp.sqrt(full)
    keep = jnp.where(waves * 2.0 < full, 1.0, 0.0)
    zc, zs = turn(waves, full, 1.0 / full)
    zc_ref[...] = zc
    zs_ref[...] = zs

    base_c, base_s = turn(
        iota((STEP, WAVES), 0).astype(F32) * waves, quarter, inv_quarter
    )
    acc_c[0:STEP, :] = base_c
    acc_s[0:STEP, :] = base_s
    for start in range(0, 88, 8):
        c, s = turn((iota((8, WAVES), 0) + start).astype(F32) * (waves * float(STEP)), quarter, inv_quarter)
        wc_ref[start : start + 8, :] = c
        ws_ref[start : start + 8, :] = s

    def fill(j, carry):
        c, s = wc_ref[pl.ds(j, 1), :], ws_ref[pl.ds(j, 1), :]
        bc, bs = acc_c[0:STEP, :], acc_s[0:STEP, :]
        rows = pl.ds(pl.multiple_of(j * STEP, STEP), STEP)
        cos_tab[rows, :] = (bc * c - bs * s).astype(BF16)
        sin_tab[rows, :] = (bs * c + bc * s).astype(BF16)
        return carry

    lax.fori_loop(0, BLOCKS, fill, 0)

    column = iota((1, CHUNK), 1)
    target = (column & 127) * 4 + (column >> 7)
    sel_ref[...] = jnp.where(iota((CHUNK, CHUNK), 0) == target, 1.0, 0.0).astype(BF16)
    points = jnp.concatenate([grid_ref[f].astype(F32) for f in range(FIELDS)], axis=0)
    points = jnp.where(iota((2 * FIELDS, WIDTH), 1) < length, points, 0.0)
    points = jnp.concatenate([points, jnp.zeros((16 - 2 * FIELDS, WIDTH), F32)], axis=0).astype(BF16)
    points = jnp.concatenate([points, jnp.zeros((16, CHUNK * CHUNKS - WIDTH), BF16)], axis=1)
    points = jnp.concatenate([points[:, CHUNK * k : CHUNK * (k + 1)] for k in range(CHUNKS)], axis=0)
    points = dot(points, sel_ref[...]).astype(BF16)
    phases = jnp.concatenate(
        [
            jnp.concatenate([points[16 * k : 16 * (k + 1), 128 * b : 128 * (b + 1)] for k in range(CHUNKS)], axis=1)
            for b in range(4)
        ],
        axis=0,
    )[:, :ACROSS]

    acc_c[...] = dot(phases, cos_tab[...])
    acc_s[...] = dot(phases, sin_tab[...])
    re, im = acc_c[48:64, :], -acc_s[48:64, :]
    for b in (2, 1, 0):
        re, im = (
            re * zc + im * zs + acc_c[16 * b : 16 * (b + 1), :],
            im * zc - re * zs - acc_s[16 * b : 16 * (b + 1), :],
        )
    for c, part in enumerate((re, im)):
        part = part * (scale * keep)
        packed = jnp.concatenate(
            [part[0:10, 128 * s : 128 * (s + 1)] for s in range(SLOTS)] + [jnp.zeros((28, 128), F32)], axis=0
        )
        send1[:, c, :] = packed.T

    def exchange(source, dest, sem, row, row_at, back):
        def one(k, carry):
            other = lax.rem(owner + k, DEVS)
            o_lat, o_fld = other // FLD, lax.rem(other, FLD)
            pltpu.make_async_remote_copy(
                src_ref=source.at[row_at(o_lat, o_fld)],
                dst_ref=dest.at[row],
                send_sem=sems.at[sem],
                recv_sem=sems.at[sem + 1],
                device_id={"lat": o_lat, "fld": o_fld},
                device_id_type=MESH,
            ).start()
            return carry

        lax.fori_loop(1, DEVS, one, 0)
        dest[row] = source[row_at(lat, fld)]

    def finish(source, dest, sem):
        some = pl.ds(0, DEVS - 1)
        pltpu.make_async_copy(dest.at[some], dest.at[some], sems.at[sem + 1]).wait()
        pltpu.make_async_copy(source.at[some], source.at[some], sems.at[sem]).wait()

    pl.semaphore_wait(barrier, DEVS - 1)
    by_owner = lambda a, b: a * FLD + b
    by_group = lambda a, b: b * LAT + a
    exchange(send1, recv1, 0, by_group(lat, fld), by_owner, 0)

    place = iota((1, LANES), 1)
    for p in range(PAIRS):
        first = fold_s_ref[2 * p, owner]
        last = leg_ref[p, :, PLACES - 1 : PLACES]
        value = jnp.concatenate(
            [leg_ref[p, :, 0 : PLACES - 1], jnp.where(iota((LAT, 128), 1) == 0, last, 0.0)], axis=1
        )
        partner = place > CUT - first
        one = jnp.where(partner, 0.0, value)
        two = jnp.where(partner, value, 0.0)
        sign_one = jnp.where((place & 1) == 1, -1.0, 1.0)
        sign_two = jnp.where(((place + first) & 1) == 1, -1.0, 1.0)
        leg4_ref[p, 0:32, :] = one.astype(BF16)
        leg4_ref[p, 32:64, :] = (one * sign_one).astype(BF16)
        leg4_ref[p, 64:96, :] = two.astype(BF16)
        leg4_ref[p, 96:128, :] = (two * sign_two).astype(BF16)
        degree = jnp.where(partner, place - 1, first + place).astype(F32)
        tau = degree * (degree + 1.0) * (1.0 / float(CUT * (CUT + 1)))
        twice = jnp.where((iota((40, ALL_FIELDS), 0) >> 1) == iota((40, ALL_FIELDS), 1), rate_ref[...], 0.0)
        rates = jnp.sum(twice, axis=1, keepdims=True)
        inv_ref[p] = 1.0 / (1.0 + rates * tau)

    rows, cols = iota((40, 64), 0), iota((40, 64), 1)
    pick = jnp.where((iota((40, 20), 0) >> 1) == iota((40, 20), 1), 1.0, 0.0)
    spread_col = iota((20, 64), 1)
    spread = jnp.where(
        ((spread_col & 7) < FIELDS) & (iota((20, 64), 0) == (spread_col >> 4) * FIELDS + (spread_col & 7)), 1.0, 0.0
    )
    to_all = dot(dot(pick, to_ref[...], HIGH), spread, HIGH)
    to_all = jnp.where((rows & 1) == ((cols >> 3) & 1), to_all, 0.0)
    pick_t = jnp.where(iota((20, 40), 0) == (iota((20, 40), 1) >> 1), 1.0, 0.0)
    half = dot(back_ref[...], pick_t, HIGH)
    back_rows = dot(pick, half, HIGH)
    back_rows = jnp.where((iota((40, 40), 0) & 1) == (iota((40, 40), 1) & 1), back_rows, 0.0)
    back_upper, back_lower = split(back_rows)
    back_two = jnp.concatenate([back_upper.astype(F32), back_lower.astype(F32)], axis=0).astype(BF16)
    spread_row = iota((64, 20), 0)
    spread_t = jnp.where(
        ((spread_row & 7) < FIELDS) & (iota((64, 20), 1) == (spread_row >> 4) * FIELDS + (spread_row & 7)), 1.0, 0.0
    )
    back_all = dot(spread_t, half, HIGH)
    back_all = jnp.where(((iota((64, 40), 0) >> 3) & 1) == (iota((64, 40), 1) & 1), back_all, 0.0)
    bands = dot(band_ref[...].astype(F32), jnp.where(iota((LAT, 128), 0) == (iota((LAT, 128), 1) & 31), 1.0, 0.0), HIGH)
    bands = jnp.round(bands).astype(I32)
    square0, square1 = iota((128, 128), 0), iota((128, 128), 1)
    perm = jnp.where(((square0 & 31) == bands) & ((square0 >> 5) == (square1 >> 5)), 1.0, 0.0)

    finish(send1, recv1, 0)

    for c in range(2):
        turned[c] = recv1[:, c, :].T
    block = iota((16, 128), 1) >> 5
    gathered = []
    for p in range(PAIRS):
        rolled = []
        for j in range(4):
            at = 10 * (2 * p + (j >> 1)) + (j & 1)
            source = jnp.concatenate([turned[c, pl.ds(at, 8, stride=2), :] for c in range(2)], axis=0)
            rolled.append([source] + [pltpu.roll(source, 32 * k, 1) for k in range(1, 4)])
        parts = []
        for g in range(FLD):
            total = rolled[0][(0 - g) % 4]
            for j in range(1, 4):
                total = jnp.where(block == j, rolled[j][(j - g) % 4], total)
            parts.append(total)
        gathered.append(jnp.concatenate(parts, axis=0))
    modes_at = dot(to_all, jnp.concatenate(gathered, axis=1), HIGH)
    modes_at = jnp.concatenate([modes_at[:, 128 * p : 128 * (p + 1)] for p in range(PAIRS)], axis=0)
    modes_at = dot_nt(modes_at.astype(BF16), perm.astype(BF16))

    sums = []
    for p in range(PAIRS):
        modes = dot(modes_at[40 * p : 40 * (p + 1)].astype(BF16), leg4_ref[p])
        damped = (modes * inv_ref[p]).astype(BF16)
        sums.append(dot_nt(damped, leg4_ref[p]))
        spec = dot(back_two, damped)
        spec = spec[0:40] + spec[40:80]
        for g in range(ALL_FIELDS):
            spec_ref[g, p, :, :] = spec[2 * g : 2 * g + 2, 0:PLACES]

    returned = dot(back_all, jnp.concatenate(sums, axis=1), HIGH)
    returned = jnp.concatenate([returned[:, 128 * p : 128 * (p + 1)] for p in range(PAIRS)], axis=0)
    returned = dot(returned, perm, HIGH)
    turned[...] = jnp.zeros_like(turned)
    for p in range(PAIRS):
        rolled = []
        for g in range(FLD):
            source = returned[64 * p + 16 * g : 64 * p + 16 * (g + 1)]
            rolled.append([source] + [pltpu.roll(source, 32 * k, 1) for k in range(1, 4)])
        for j in range(4):
            total = rolled[0][(0 - j) % 4]
            for g in range(1, 4):
                total = jnp.where(block == g, rolled[g][(g - j) % 4], total)
            at = 10 * (2 * p + (j >> 1)) + (j & 1)
            for c in range(2):
                turned[c, pl.ds(at, 8, stride=2), :] = total[8 * c : 8 * (c + 1)]
    for c in range(2):
        send2[:, c, :] = turned[c].T
    exchange(send2, recv2, 2, by_owner(lat, fld), by_group, 0)
    finish(send2, recv2, 2)

    for c in range(2):
        turned[c] = recv2[:, c, :].T
    zc, zs = zc_ref[...], zs_ref[...]
    weight = keep * jnp.where(waves == 0.0, 1.0, 2.0)
    re, im = (
        jnp.concatenate([turned[c, 10 * s : 10 * s + 16, :] for s in range(SLOTS)], axis=1) * weight for c in range(2)
    )
    res, ims = [re], [im]
    for b in range(1, 4):
        re, im = re * zc - im * zs, re * zs + im * zc
        res.append(re)
        ims.append(im)
    total = dot_nt(jnp.concatenate(res, axis=0).astype(BF16), cos_tab[...])
    total = total - dot_nt(jnp.concatenate(ims, axis=0).astype(BF16), sin_tab[...])
    total = total * scale[:, 0:1]
    total = jnp.where(iota((64, ACROSS), 1) * 4 < length, total, 0.0)
    total = jnp.concatenate([total, jnp.zeros((64, LANES - ACROSS), F32)], axis=1).astype(BF16)
    total = jnp.concatenate(
        [
            jnp.concatenate([total[16 * b : 16 * (b + 1), 128 * k : 128 * (k + 1)] for b in range(4)], axis=1)
            for k in range(CHUNKS)
        ],
        axis=0,
    )
    total = dot_nt(total, sel_ref[...])
    total = jnp.concatenate([total[16 * k : 16 * (k + 1)] for k in range(CHUNKS)], axis=1)[:, :WIDTH]
    for f in range(FIELDS):
        out_ref[f, :, :] = total[2 * f : 2 * f + 2].astype(BF16)


def per_device(grid, row_lengths, band_map, fold_map, legendre, to_modes, back_modes, mode_rates):
    smem = pl.BlockSpec(memory_space=pltpu.SMEM)
    vmem = pl.BlockSpec(memory_space=pltpu.VMEM)
    fold_t = fold_map.T
    spectral, grid_out = pl.pallas_call(
        kernel,
        out_shape=(
            jax.ShapeDtypeStruct((ALL_FIELDS, PAIRS, 2, PLACES), F32),
            jax.ShapeDtypeStruct((FIELDS, 2, WIDTH), BF16),
        ),
        in_specs=[smem] * 3 + [vmem] * 7,
        out_specs=(vmem, vmem),
        scratch_shapes=[
            pltpu.VMEM((ACROSS, WAVES), BF16),
            pltpu.VMEM((ACROSS, WAVES), BF16),
            pltpu.VMEM((88, WAVES), F32),
            pltpu.VMEM((88, WAVES), F32),
            pltpu.VMEM((CHUNK, CHUNK), BF16),
            pltpu.VMEM((PAIRS, 128, LANES), BF16),
            pltpu.VMEM((PAIRS, 40, LANES), F32),
            pltpu.VMEM((64, WAVES), F32),
            pltpu.VMEM((64, WAVES), F32),
            pltpu.VMEM((1, WAVES), F32),
            pltpu.VMEM((1, WAVES), F32),
            pltpu.VMEM((8, 128), F32),
            pltpu.VMEM((128, 128), F32),
            pltpu.VMEM((2, 128, 128), F32),
            pltpu.VMEM((DEVS, 2, 128), F32),
            pltpu.VMEM((DEVS, 2, 128), F32),
            pltpu.VMEM((DEVS, 2, 128), F32),
            pltpu.VMEM((DEVS, 2, 128), F32),
            pltpu.SemaphoreType.DMA((4,)),
        ],
        compiler_params=pltpu.CompilerParams(
            collective_id=0, has_side_effects=True, vmem_limit_bytes=56 * 1024 * 1024
        ),
        name="spectral_transform",
    )(
        row_lengths,
        band_map,
        fold_t,
        fold_t,
        band_map.reshape(1, LAT),
        grid.reshape(FIELDS, 2, WIDTH),
        jnp.transpose(legendre, (0, 2, 1)),
        to_modes,
        back_modes,
        mode_rates.reshape(1, ALL_FIELDS),
    )
    return jnp.transpose(spectral, (0, 2, 1, 3)), grid_out.reshape(FIELDS, 1, 2, WIDTH)


def solution(mesh):
    placed = (
        P("fld", "lat", None, None),
        P(),
        P(),
        P(),
        P(("lat", "fld"), None, None),
        P(),
        P(),
        P(),
    )
    return jax.shard_map(
        per_device,
        mesh=mesh,
        in_specs=placed,
        out_specs=(P(None, None, ("lat", "fld"), None), P("fld", "lat", None, None)),
        check_vma=False,
    )
```

```python
import functools
import math

import jax
import jax.numpy as jnp
from jax import lax
from jax.experimental import pallas as pl
from jax.experimental.pallas import tpu as pltpu
from jax.sharding import PartitionSpec as P

HIGH = lax.Precision.HIGHEST
MESH = pl.DeviceIdType.MESH
F32, BF16, I32 = jnp.float32, jnp.bfloat16, jnp.int32
NT = (((1,), (1,)), ((), ()))

LAT, FLD = 32, 4
DEVS = LAT * FLD
FIELDS = 5
ALL_FIELDS = FIELDS * FLD
SLOTS = 10
PAIRS = SLOTS // 2
PLACES = 1281
CUT = 1279
WIDTH = 5248
WAVES = DEVS * SLOTS
ACROSS = 1296
STEP = 16
BLOCKS = ACROSS // STEP
LANES = 1408
CHUNK = 512
CHUNKS = 11


def iota(shape, dim):
    return lax.broadcasted_iota(I32, shape, dim)


def dot(a, b, precision=None):
    return jnp.dot(a, b, precision=precision, preferred_element_type=F32)


def dot_nt(a, b):
    return lax.dot_general(a, b, NT, preferred_element_type=F32)


SIN_TERMS = [(-1) ** k * math.pi ** (2 * k + 1) / math.factorial(2 * k + 1) for k in range(6)]
COS_TERMS = [(-1) ** k * math.pi ** (2 * k) / math.factorial(2 * k) for k in range(7)]


def horner(terms, square):
    total = jnp.full_like(square, terms[-1])
    for term in terms[-2::-1]:
        total = total * square + term
    return total


def turn(product, period, inverse):
    rest = product - period * jnp.round(product * inverse)
    part = rest * inverse
    square = part * part
    half_sin = part * horner(SIN_TERMS, square)
    half_cos = horner(COS_TERMS, square)
    return 1.0 - 2.0 * half_sin * half_sin, 2.0 * half_sin * half_cos


def row_of(value):
    return jnp.concatenate([value[s : s + 1] for s in range(SLOTS)], axis=1)


def split(value):
    upper = value.astype(BF16)
    return upper, (value - upper.astype(F32)).astype(BF16)


def offsets():
    hops = (0, 1, 2, 1)
    steps = [(x, y, z, c) for y in range(4) for z in range(4) for c in range(2) for x in range(4)][1:]
    return sorted(steps, key=lambda step: -(hops[step[0]] + hops[step[1]] + hops[step[2]]))


def send_kernel(
    len_hbm, band_s_hbm, fold_hbm, band_hbm, grid_hbm, leg_hbm, to_hbm, back_hbm, rate_hbm,
    spec_ref, cos_tab, sin_tab, tre_ref, tim_ref, size_ref,
    len_ref, band_s_ref, fold_s_ref, fold_ref, band_ref, grid_ref, leg_ref, to_ref, back_ref, rate_ref,
    wc_ref, ws_ref, leg4_ref, inv_ref, damp_ref, acc_c, acc_s, turned,
    send1, recv1, send2, recv2, in_sems, sems,
):
    lat = lax.axis_index("lat")
    fld = lax.axis_index("fld")
    owner = lat * FLD + fld

    moves = [
        pltpu.make_async_copy(source, dest, in_sems.at[k])
        for k, (source, dest) in enumerate(
            (
                (len_hbm, len_ref), (band_s_hbm, band_s_ref), (fold_hbm, fold_ref), (grid_hbm, grid_ref),
                (fold_hbm, fold_s_ref), (band_hbm, band_ref), (to_hbm, to_ref), (back_hbm, back_ref),
                (rate_hbm, rate_ref), (leg_hbm, leg_ref),
            )
        )
    ]
    for move in moves:
        move.start()

    high, middle, core = lat // 8, lax.rem(lat // 2, 4), lax.rem(lat, 2)
    xs, ys, zs_, cs = (
        [at] + [lax.rem(at + k, size) for k in range(1, size)]
        for at, size in ((fld, 4), (high, 4), (middle, 4), (core, 2))
    )
    peers = [(ys[y] * 8 + zs_[z] * 2 + cs[c], xs[x]) for x, y, z, c in offsets()]

    barrier = pltpu.get_barrier_semaphore()
    for o_lat, o_fld in peers:
        pl.semaphore_signal(barrier, inc=1, device_id={"lat": o_lat, "fld": o_fld}, device_id_type=MESH)

    for move in moves[:4]:
        move.wait()
    length = len_ref[band_s_ref[lat]]
    waves = row_of(fold_ref[...].astype(F32))
    full = jnp.full((1, WAVES), length.astype(F32), F32)
    size_ref[...] = jnp.full((8, 128), length.astype(F32), F32)
    quarter = full * 0.25
    inv_quarter = 1.0 / quarter
    scale = 1.0 / jnp.sqrt(full)
    keep = jnp.where(waves * 2.0 < full, 1.0, 0.0)
    zc, zs = turn(waves, full, 1.0 / full)

    base_c, base_s = turn(
        iota((STEP, WAVES), 0).astype(F32) * waves, quarter, inv_quarter
    )
    acc_c[0:STEP, :] = base_c
    acc_s[0:STEP, :] = base_s
    for start in range(0, 88, 8):
        c, s = turn((iota((8, WAVES), 0) + start).astype(F32) * (waves * float(STEP)), quarter, inv_quarter)
        wc_ref[start : start + 8, :] = c
        ws_ref[start : start + 8, :] = s

    def fill(j, carry):
        c, s = wc_ref[pl.ds(j, 1), :], ws_ref[pl.ds(j, 1), :]
        bc, bs = acc_c[0:STEP, :], acc_s[0:STEP, :]
        rows = pl.ds(pl.multiple_of(j * STEP, STEP), STEP)
        cos_tab[rows, :] = (bc * c - bs * s).astype(BF16)
        sin_tab[rows, :] = (bs * c + bc * s).astype(BF16)
        return carry

    lax.fori_loop(0, BLOCKS, fill, 0)

    points = jnp.concatenate([grid_ref[f].astype(F32) for f in range(FIELDS)], axis=0)
    points = jnp.where(iota((2 * FIELDS, WIDTH), 1) < length, points, 0.0)
    points = jnp.concatenate([points, jnp.zeros((16 - 2 * FIELDS, WIDTH), F32)], axis=0).astype(BF16)
    points = jnp.concatenate([points, jnp.zeros((16, CHUNK * CHUNKS - WIDTH), BF16)], axis=1)
    points = jnp.concatenate([points[:, CHUNK * k : CHUNK * (k + 1)] for k in range(CHUNKS)], axis=0)
    points = dot(points, selection()).astype(BF16)
    phases = jnp.concatenate(
        [
            jnp.concatenate([points[16 * k : 16 * (k + 1), 128 * b : 128 * (b + 1)] for k in range(CHUNKS)], axis=1)
            for b in range(4)
        ],
        axis=0,
    )[:, :ACROSS]

    acc_c[...] = dot(phases, cos_tab[...])
    acc_s[...] = dot(phases, sin_tab[...])
    re, im = acc_c[48:64, :], -acc_s[48:64, :]
    for b in (2, 1, 0):
        re, im = (
            re * zc + im * zs + acc_c[16 * b : 16 * (b + 1), :],
            im * zc - re * zs - acc_s[16 * b : 16 * (b + 1), :],
        )
    for c, part in enumerate((re, im)):
        part = part * (scale * keep)
        packed = jnp.concatenate(
            [part[0:10, 128 * s : 128 * (s + 1)] for s in range(SLOTS)] + [jnp.zeros((28, 128), F32)], axis=0
        )
        send1[:, c, :] = packed.T

    for move in moves[4:]:
        move.wait()
    perm = jnp.where(iota((LAT, LAT), 0) == band_ref[...], 1.0, 0.0).astype(BF16)
    rates = jnp.sum(
        jnp.where((iota((40, ALL_FIELDS), 0) >> 1) == iota((40, ALL_FIELDS), 1), rate_ref[...], 0.0),
        axis=1, keepdims=True,
    )
    place = iota((1, LANES), 1)
    for p in range(PAIRS):
        first = fold_s_ref[2 * p, owner]
        last = leg_ref[p, :, PLACES - 1 : PLACES]
        value = jnp.concatenate(
            [leg_ref[p, :, 0 : PLACES - 1], jnp.where(iota((LAT, 128), 1) == 0, last, 0.0)], axis=1
        )
        value = lax.dot_general(perm, value.astype(BF16), (((0,), (0,)), ((), ())), preferred_element_type=F32)
        partner = place > CUT - first
        one = jnp.where(partner, 0.0, value)
        two = jnp.where(partner, value, 0.0)
        sign_one = jnp.where((place & 1) == 1, -1.0, 1.0)
        sign_two = jnp.where(((place + first) & 1) == 1, -1.0, 1.0)
        leg4_ref[p, 0:32, :] = one.astype(BF16)
        leg4_ref[p, 32:64, :] = (one * sign_one).astype(BF16)
        leg4_ref[p, 64:96, :] = two.astype(BF16)
        leg4_ref[p, 96:128, :] = (two * sign_two).astype(BF16)
        degree = jnp.where(partner, place - 1, first + place).astype(F32)
        tau = degree * (degree + 1.0) * (1.0 / float(CUT * (CUT + 1)))
        inv_ref[p] = 1.0 / (1.0 + rates * tau)

    rows, cols = iota((40, 64), 0), iota((40, 64), 1)
    pick = jnp.where((iota((40, 20), 0) >> 1) == iota((40, 20), 1), 1.0, 0.0)
    spread_col = iota((20, 64), 1)
    spread = jnp.where(
        ((spread_col & 7) < FIELDS) & (iota((20, 64), 0) == (spread_col >> 4) * FIELDS + (spread_col & 7)), 1.0, 0.0
    )
    to_all = dot(dot(pick, to_ref[...], HIGH), spread, HIGH)
    to_all = jnp.where((rows & 1) == ((cols >> 3) & 1), to_all, 0.0)
    pick_t = jnp.where(iota((20, 40), 0) == (iota((20, 40), 1) >> 1), 1.0, 0.0)
    half = dot(back_ref[...], pick_t, HIGH)
    back_rows = dot(pick, half, HIGH)
    back_rows = jnp.where((iota((40, 40), 0) & 1) == (iota((40, 40), 1) & 1), back_rows, 0.0)
    back_upper, back_lower = split(back_rows)
    back_two = jnp.concatenate([back_upper.astype(F32), back_lower.astype(F32)], axis=0).astype(BF16)
    spread_row = iota((64, 20), 0)
    spread_t = jnp.where(
        ((spread_row & 7) < FIELDS) & (iota((64, 20), 1) == (spread_row >> 4) * FIELDS + (spread_row & 7)), 1.0, 0.0
    )
    back_all = dot(spread_t, half, HIGH)
    back_all = jnp.where(((iota((64, 40), 0) >> 3) & 1) == (iota((64, 40), 1) & 1), back_all, 0.0)

    def exchange(source, dest, sem, row, row_at):
        for o_lat, o_fld in peers:
            pltpu.make_async_remote_copy(
                src_ref=source.at[row_at(o_lat, o_fld)],
                dst_ref=dest.at[row],
                send_sem=sems.at[sem],
                recv_sem=sems.at[sem + 1],
                device_id={"lat": o_lat, "fld": o_fld},
                device_id_type=MESH,
            ).start()
        dest[row] = source[row_at(lat, fld)]

    def finish(buffer, sem):
        some = buffer.at[pl.ds(0, DEVS - 1)]
        pltpu.make_async_copy(some, some, sems.at[sem]).wait()

    by_owner = lambda a, b: a * FLD + b
    by_group = lambda a, b: b * LAT + a
    pl.semaphore_wait(barrier, DEVS - 1)
    exchange(send1, recv1, 0, by_group(lat, fld), by_owner)
    finish(recv1, 1)

    for c in range(2):
        turned[c] = recv1[:, c, :].T
    block = iota((16, 128), 1) >> 5
    gathered = []
    for p in range(PAIRS):
        rolled = []
        for j in range(4):
            at = 10 * (2 * p + (j >> 1)) + (j & 1)
            source = jnp.concatenate([turned[c, pl.ds(at, 8, stride=2), :] for c in range(2)], axis=0)
            rolled.append([source] + [pltpu.roll(source, 32 * k, 1) for k in range(1, 4)])
        parts = []
        for g in range(FLD):
            total = rolled[0][(0 - g) % 4]
            for j in range(1, 4):
                total = jnp.where(block == j, rolled[j][(j - g) % 4], total)
            parts.append(total)
        gathered.append(jnp.concatenate(parts, axis=0))
    modes_at = dot(to_all, jnp.concatenate(gathered, axis=1), HIGH).astype(BF16)

    sums = []
    for p in range(PAIRS):
        modes = dot(modes_at[:, 128 * p : 128 * (p + 1)], leg4_ref[p])
        damped = (modes * inv_ref[p]).astype(BF16)
        damp_ref[p, 0:40, :] = damped
        sums.append(dot_nt(damped, leg4_ref[p]))

    returned = dot(back_all, jnp.concatenate(sums, axis=1), HIGH)
    turned[...] = jnp.zeros_like(turned)
    for p in range(PAIRS):
        rolled = []
        for g in range(FLD):
            source = returned[16 * g : 16 * (g + 1), 128 * p : 128 * (p + 1)]
            rolled.append([source] + [pltpu.roll(source, 32 * k, 1) for k in range(1, 4)])
        for j in range(4):
            total = rolled[0][(0 - j) % 4]
            for g in range(1, 4):
                total = jnp.where(block == g, rolled[g][(g - j) % 4], total)
            at = 10 * (2 * p + (j >> 1)) + (j & 1)
            for c in range(2):
                turned[c, pl.ds(at, 8, stride=2), :] = total[8 * c : 8 * (c + 1)]
    for c in range(2):
        send2[:, c, :] = turned[c].T
    exchange(send2, recv2, 2, by_owner(lat, fld), by_group)

    for p in range(PAIRS):
        spec = dot(back_two, damp_ref[p, 0:40, :])
        spec = spec[0:40] + spec[40:80]
        for g in range(ALL_FIELDS):
            spec_ref[g, p, :, :] = spec[2 * g : 2 * g + 2, 0:PLACES]

    finish(recv2, 3)

    for c in range(2):
        turned[c] = recv2[:, c, :].T
    weight = keep * jnp.where(waves == 0.0, 1.0, 2.0)
    re, im = (
        jnp.concatenate([turned[c, 10 * s : 10 * s + 16, :] for s in range(SLOTS)], axis=1) * weight for c in range(2)
    )
    for b in range(4):
        tre_ref[16 * b : 16 * (b + 1), :] = re.astype(BF16)
        tim_ref[16 * b : 16 * (b + 1), :] = im.astype(BF16)
        if b < 3:
            re, im = re * zc - im * zs, re * zs + im * zc
    finish(send1, 0)
    finish(send2, 2)


def points_kernel(spec_in, cos_tab, sin_tab, tre_ref, tim_ref, size_ref, spec_out, out_ref, sem):
    move = pltpu.make_async_copy(spec_in, spec_out, sem)
    move.start()
    length = size_ref[0:1, 0:1]
    scale = 1.0 / jnp.sqrt(length)
    total = dot_nt(tre_ref[...], cos_tab[...]) - dot_nt(tim_ref[...], sin_tab[...])
    total = total * scale
    total = jnp.where((iota((64, ACROSS), 1) * 4).astype(F32) < length, total, 0.0)
    total = jnp.concatenate([total, jnp.zeros((64, LANES - ACROSS), F32)], axis=1).astype(BF16)
    total = jnp.concatenate(
        [
            jnp.concatenate([total[16 * b : 16 * (b + 1), 128 * k : 128 * (k + 1)] for b in range(4)], axis=1)
            for k in range(CHUNKS)
        ],
        axis=0,
    )
    total = dot_nt(total, selection())
    total = jnp.concatenate([total[16 * k : 16 * (k + 1)] for k in range(CHUNKS)], axis=1)[:, :WIDTH]
    for f in range(FIELDS):
        out_ref[f, :, :] = total[2 * f : 2 * f + 2].astype(BF16)
    move.wait()


def selection():
    column = iota((1, CHUNK), 1)
    target = (column & 127) * 4 + (column >> 7)
    return jnp.where(iota((CHUNK, CHUNK), 0) == target, 1.0, 0.0).astype(BF16)


def per_device(grid, row_lengths, band_map, fold_map, legendre, to_modes, back_modes, mode_rates):
    vmem = pl.BlockSpec(memory_space=pltpu.VMEM)
    anywhere = pl.BlockSpec(memory_space=pl.ANY)
    spec_shape = (ALL_FIELDS, PAIRS, 2, PLACES)
    held = pl.pallas_call(
        send_kernel,
        out_shape=(
            pltpu.VMEM(spec_shape, F32),
            pltpu.VMEM((ACROSS, WAVES), BF16),
            pltpu.VMEM((ACROSS, WAVES), BF16),
            pltpu.VMEM((64, WAVES), BF16),
            pltpu.VMEM((64, WAVES), BF16),
            pltpu.VMEM((8, 128), F32),
        ),
        in_specs=[pl.BlockSpec(memory_space=pltpu.HBM)] * 9,
        out_specs=(vmem,) * 6,
        scratch_shapes=[
            pltpu.SMEM((LAT,), I32),
            pltpu.SMEM((LAT,), I32),
            pltpu.SMEM((SLOTS, DEVS), I32),
            pltpu.VMEM((SLOTS, DEVS), I32),
            pltpu.VMEM((1, LAT), I32),
            pltpu.VMEM((FIELDS, 2, WIDTH), BF16),
            pltpu.VMEM((PAIRS, LAT, PLACES), F32),
            pltpu.VMEM((ALL_FIELDS, ALL_FIELDS), F32),
            pltpu.VMEM((ALL_FIELDS, ALL_FIELDS), F32),
            pltpu.VMEM((1, ALL_FIELDS), F32),
            pltpu.VMEM((88, WAVES), F32),
            pltpu.VMEM((88, WAVES), F32),
            pltpu.VMEM((PAIRS, 128, LANES), BF16),
            pltpu.VMEM((PAIRS, 40, LANES), F32),
            pltpu.VMEM((PAIRS, 48, LANES), BF16),
            pltpu.VMEM((64, WAVES), F32),
            pltpu.VMEM((64, WAVES), F32),
            pltpu.VMEM((2, 128, 128), F32),
            pltpu.VMEM((DEVS, 2, 128), F32),
            pltpu.VMEM((DEVS, 2, 128), F32),
            pltpu.VMEM((DEVS, 2, 128), F32),
            pltpu.VMEM((DEVS, 2, 128), F32),
            pltpu.SemaphoreType.DMA((10,)),
            pltpu.SemaphoreType.DMA((4,)),
        ],
        compiler_params=pltpu.CompilerParams(
            collective_id=0, has_side_effects=True, vmem_limit_bytes=24 * 1024 * 1024
        ),
        name="to_spectral",
    )(
        *[
            pltpu.with_memory_space_constraint(value, pltpu.HBM)
            for value in (
                row_lengths,
                band_map,
                fold_map.T,
                band_map.reshape(1, LAT),
                grid.reshape(FIELDS, 2, WIDTH),
                jnp.transpose(legendre, (0, 2, 1)),
                to_modes,
                back_modes,
                mode_rates.reshape(1, ALL_FIELDS),
            )
        ]
    )
    held = [pltpu.with_memory_space_constraint(value, pltpu.VMEM) for value in held]
    spectral, grid_out = pl.pallas_call(
        points_kernel,
        out_shape=(
            jax.ShapeDtypeStruct(spec_shape, F32),
            jax.ShapeDtypeStruct((FIELDS, 2, WIDTH), BF16),
        ),
        in_specs=[vmem] * 6,
        out_specs=(anywhere, vmem),
        scratch_shapes=[pltpu.SemaphoreType.DMA],
        compiler_params=pltpu.CompilerParams(vmem_limit_bytes=24 * 1024 * 1024),
        name="to_points",
    )(*held)
    return jnp.transpose(spectral, (0, 2, 1, 3)), grid_out.reshape(FIELDS, 1, 2, WIDTH)


def solution(mesh):
    placed = (
        P("fld", "lat", None, None),
        P(),
        P(),
        P(),
        P(("lat", "fld"), None, None),
        P(),
        P(),
        P(),
    )
    return jax.shard_map(
        per_device,
        mesh=mesh,
        in_specs=placed,
        out_specs=(P(None, None, ("lat", "fld"), None), P("fld", "lat", None, None)),
        check_vma=False,
    )
```

```python
import functools
import math

import jax
import jax.numpy as jnp
from jax import lax
from jax.experimental import pallas as pl
from jax.experimental.pallas import tpu as pltpu
from jax.sharding import PartitionSpec as P

HIGH = lax.Precision.HIGHEST
MESH = pl.DeviceIdType.MESH
F32, BF16, I32 = jnp.float32, jnp.bfloat16, jnp.int32
NT = (((1,), (1,)), ((), ()))

LAT, FLD = 32, 4
DEVS = LAT * FLD
FIELDS = 5
ALL_FIELDS = FIELDS * FLD
SLOTS = 10
PAIRS = SLOTS // 2
PLACES = 1281
CUT = 1279
WIDTH = 5248
WAVES = DEVS * SLOTS
HALF = 672
GROUP = 256
UNROLL = 2
STEP = 16
BLOCKS = HALF // STEP
LANES = 1408
CHUNK = 512
CHUNKS = 11


def iota(shape, dim):
    return lax.broadcasted_iota(I32, shape, dim)


def dot(a, b, precision=None):
    return jnp.dot(a, b, precision=precision, preferred_element_type=F32)


def dot_nt(a, b):
    return lax.dot_general(a, b, NT, preferred_element_type=F32)


SIN_TERMS = [(-1) ** k * math.pi ** (2 * k + 1) / math.factorial(2 * k + 1) for k in range(6)]
COS_TERMS = [(-1) ** k * math.pi ** (2 * k) / math.factorial(2 * k) for k in range(7)]


def horner(terms, square):
    total = jnp.full_like(square, terms[-1])
    for term in terms[-2::-1]:
        total = total * square + term
    return total


def turn(product, period, inverse):
    rest = product - period * jnp.round(product * inverse)
    part = rest * inverse
    square = part * part
    half_sin = part * horner(SIN_TERMS, square)
    half_cos = horner(COS_TERMS, square)
    return 1.0 - 2.0 * half_sin * half_sin, 2.0 * half_sin * half_cos


def row_of(value):
    return jnp.concatenate([value[s : s + 1] for s in range(SLOTS)], axis=1)


def split(value):
    upper = value.astype(BF16)
    return upper, (value - upper.astype(F32)).astype(BF16)


def dot_split(left, right):
    left_upper, left_lower = split(left)
    right_upper, right_lower = split(right)
    return dot(left_upper, right_upper) + (dot(left_upper, right_lower) + dot(left_lower, right_upper))


def offsets():
    hops = (0, 1, 2, 1)
    steps = [(x, y, z, c) for y in range(4) for z in range(4) for c in range(2) for x in range(4)][1:]
    return sorted(steps, key=lambda step: -(hops[step[0]] + hops[step[1]] + hops[step[2]]))


def send_kernel(
    len_hbm, band_s_hbm, fold_hbm, band_hbm, grid_hbm, leg_hbm, to_hbm, back_hbm, rate_hbm,
    spec_ref, cos_tab, sin_tab, tre_ref, tim_ref, size_ref, sel_ref,
    len_ref, band_s_ref, fold_s_ref, fold_ref, band_ref, grid_ref, leg_ref, to_ref, back_ref, rate_ref,
    wc_ref, ws_ref, rev_ref, leg4_ref, inv_ref, damp_ref, acc_c, acc_s, turned,
    send1, recv1, send2, recv2, in_sems, sems,
):
    lat = lax.axis_index("lat")
    fld = lax.axis_index("fld")
    owner = lat * FLD + fld

    moves = [
        pltpu.make_async_copy(source, dest, in_sems.at[k])
        for k, (source, dest) in enumerate(
            (
                (len_hbm, len_ref), (band_s_hbm, band_s_ref), (fold_hbm, fold_ref), (grid_hbm, grid_ref),
                (fold_hbm, fold_s_ref), (band_hbm, band_ref), (to_hbm, to_ref), (back_hbm, back_ref),
                (rate_hbm, rate_ref), (leg_hbm, leg_ref),
            )
        )
    ]
    for move in moves:
        move.start()

    high, middle, core = lat // 8, lax.rem(lat // 2, 4), lax.rem(lat, 2)
    xs, ys, zs_, cs = (
        [at] + [lax.rem(at + k, size) for k in range(1, size)]
        for at, size in ((fld, 4), (high, 4), (middle, 4), (core, 2))
    )
    peers = [(ys[y] * 8 + zs_[z] * 2 + cs[c], xs[x]) for x, y, z, c in offsets()]

    barrier = pltpu.get_barrier_semaphore()
    for o_lat, o_fld in peers:
        pl.semaphore_signal(barrier, inc=1, device_id={"lat": o_lat, "fld": o_fld}, device_id_type=MESH)

    sel_ref[...] = selection(False)
    rev_ref[...] = selection(True)

    for move in moves[:4]:
        move.wait()
    length = len_ref[band_s_ref[lat]]
    waves = row_of(fold_ref[...].astype(F32))
    full = jnp.full((1, WAVES), length.astype(F32), F32)
    size_ref[...] = jnp.full((8, 128), length, I32)
    quarter = full * 0.25
    inv_quarter = 1.0 / quarter
    scale = 1.0 / jnp.sqrt(full)
    keep = jnp.where(waves * 2.0 < full, 1.0, 0.0)
    zc, zs = turn(waves, full, 1.0 / full)

    base_c, base_s = turn(iota((STEP, WAVES), 0).astype(F32) * waves, quarter, inv_quarter)
    for start in range(0, 48, 8):
        c, s = turn((iota((8, WAVES), 0) + start).astype(F32) * (waves * float(STEP)), quarter, inv_quarter)
        wc_ref[start : start + 8, :] = c
        ws_ref[start : start + 8, :] = s
    for start in range(0, WAVES, GROUP):
        lanes = slice(start, start + GROUP)
        bc, bs = base_c[:, lanes], base_s[:, lanes]

        def fill(j, carry):
            c, s = wc_ref[pl.ds(j, 1), lanes], ws_ref[pl.ds(j, 1), lanes]
            rows = pl.ds(pl.multiple_of(j * STEP, STEP), STEP)
            cos_tab[rows, lanes] = (bc * c - bs * s).astype(BF16)
            sin_tab[rows, lanes] = (bs * c + bc * s).astype(BF16)
            return carry

        lax.fori_loop(0, BLOCKS, fill, 0, unroll=UNROLL)

    points = jnp.concatenate([grid_ref[f].astype(F32) for f in range(FIELDS)], axis=0)
    points = jnp.where(iota((2 * FIELDS, WIDTH), 1) < length, points, 0.0)
    points = jnp.concatenate([points, jnp.zeros((16 - 2 * FIELDS, WIDTH), F32)], axis=0).astype(BF16)
    points = jnp.concatenate([points, jnp.zeros((16, CHUNK * CHUNKS - WIDTH), BF16)], axis=1)
    points = jnp.concatenate([points[:, CHUNK * k : CHUNK * (k + 1)] for k in range(CHUNKS)], axis=0)

    def by_phase(values, order):
        return jnp.concatenate(
            [
                jnp.concatenate([values[16 * k : 16 * (k + 1), 128 * b : 128 * (b + 1)] for k in order], axis=1)
                for b in range(4)
            ],
            axis=0,
        )

    ahead = by_phase(dot(points, sel_ref[...]), range(6))[:, :HALF]
    behind = by_phase(dot(points, rev_ref[...]), range(CHUNKS - 1, -1, -1))
    behind = pltpu.roll(behind, length // 4 + 1, 1)[:, :HALF]
    twice = (iota((64, HALF), 1) * 8).astype(F32)
    whole = full[:, :HALF]
    share = jnp.where(twice < whole, 1.0, jnp.where(twice == whole, 0.5, 0.0))

    acc_c[...] = dot(((ahead + behind) * share).astype(BF16), cos_tab[...])
    acc_s[...] = dot(((ahead - behind) * share).astype(BF16), sin_tab[...])
    re, im = acc_c[48:64, :], -acc_s[48:64, :]
    for b in (2, 1, 0):
        re, im = (
            re * zc + im * zs + acc_c[16 * b : 16 * (b + 1), :],
            im * zc - re * zs - acc_s[16 * b : 16 * (b + 1), :],
        )
    for c, part in enumerate((re, im)):
        part = part * (scale * keep)
        packed = jnp.concatenate(
            [part[0:10, 128 * s : 128 * (s + 1)] for s in range(SLOTS)] + [jnp.zeros((28, 128), F32)], axis=0
        )
        send1[:, c, :] = packed.T

    def exchange(source, dest, sem, row, row_at):
        for o_lat, o_fld in peers:
            pltpu.make_async_remote_copy(
                src_ref=source.at[row_at(o_lat, o_fld)],
                dst_ref=dest.at[row],
                send_sem=sems.at[sem],
                recv_sem=sems.at[sem + 1],
                device_id={"lat": o_lat, "fld": o_fld},
                device_id_type=MESH,
            ).start()
        dest[row] = source[row_at(lat, fld)]

    def finish(buffer, sem):
        some = buffer.at[pl.ds(0, DEVS - 1)]
        pltpu.make_async_copy(some, some, sems.at[sem]).wait()

    by_owner = lambda a, b: a * FLD + b
    by_group = lambda a, b: b * LAT + a
    pl.semaphore_wait(barrier, DEVS - 1)
    exchange(send1, recv1, 0, by_group(lat, fld), by_owner)

    for move in moves[4:]:
        move.wait()
    perm = jnp.where(iota((LAT, LAT), 0) == band_ref[...], 1.0, 0.0).astype(BF16)
    rates = jnp.sum(
        jnp.where((iota((40, ALL_FIELDS), 0) >> 1) == iota((40, ALL_FIELDS), 1), rate_ref[...], 0.0),
        axis=1, keepdims=True,
    )
    place = iota((1, LANES), 1)
    for p in range(PAIRS):
        first = fold_s_ref[2 * p, owner]
        last = leg_ref[p, :, PLACES - 1 : PLACES]
        value = jnp.concatenate(
            [leg_ref[p, :, 0 : PLACES - 1], jnp.where(iota((LAT, 128), 1) == 0, last, 0.0)], axis=1
        )
        value = lax.dot_general(perm, value.astype(BF16), (((0,), (0,)), ((), ())), preferred_element_type=F32)
        partner = place > CUT - first
        one = jnp.where(partner, 0.0, value)
        two = jnp.where(partner, value, 0.0)
        sign_one = jnp.where((place & 1) == 1, -1.0, 1.0)
        sign_two = jnp.where(((place + first) & 1) == 1, -1.0, 1.0)
        leg4_ref[p, 0:32, :] = one.astype(BF16)
        leg4_ref[p, 32:64, :] = (one * sign_one).astype(BF16)
        leg4_ref[p, 64:96, :] = two.astype(BF16)
        leg4_ref[p, 96:128, :] = (two * sign_two).astype(BF16)
        degree = jnp.where(partner, place - 1, first + place).astype(F32)
        tau = degree * (degree + 1.0) * (1.0 / float(CUT * (CUT + 1)))
        inv_ref[p] = 1.0 / (1.0 + rates * tau)

    rows, cols = iota((40, 64), 0), iota((40, 64), 1)
    pick = jnp.where((iota((40, 20), 0) >> 1) == iota((40, 20), 1), 1.0, 0.0)
    spread_col = iota((20, 64), 1)
    spread = jnp.where(
        ((spread_col & 7) < FIELDS) & (iota((20, 64), 0) == (spread_col >> 4) * FIELDS + (spread_col & 7)), 1.0, 0.0
    )
    to_all = dot(dot(pick, to_ref[...], HIGH), spread, HIGH)
    to_all = jnp.where((rows & 1) == ((cols >> 3) & 1), to_all, 0.0)
    pick_t = jnp.where(iota((20, 40), 0) == (iota((20, 40), 1) >> 1), 1.0, 0.0)
    half = dot(back_ref[...], pick_t, HIGH)
    back_rows = dot(pick, half, HIGH)
    back_rows = jnp.where((iota((40, 40), 0) & 1) == (iota((40, 40), 1) & 1), back_rows, 0.0)
    back_upper, back_lower = split(back_rows)
    back_two = jnp.concatenate([back_upper.astype(F32), back_lower.astype(F32)], axis=0).astype(BF16)
    spread_row = iota((64, 20), 0)
    spread_t = jnp.where(
        ((spread_row & 7) < FIELDS) & (iota((64, 20), 1) == (spread_row >> 4) * FIELDS + (spread_row & 7)), 1.0, 0.0
    )
    back_all = dot(spread_t, half, HIGH)
    back_all = jnp.where(((iota((64, 40), 0) >> 3) & 1) == (iota((64, 40), 1) & 1), back_all, 0.0)

    finish(recv1, 1)

    for c in range(2):
        turned[c] = recv1[:, c, :].T
    block = iota((16, 128), 1) >> 5
    gathered = []
    for p in range(PAIRS):
        rolled = []
        for j in range(4):
            at = 10 * (2 * p + (j >> 1)) + (j & 1)
            source = jnp.concatenate([turned[c, pl.ds(at, 8, stride=2), :] for c in range(2)], axis=0)
            rolled.append([source] + [pltpu.roll(source, 32 * k, 1) for k in range(1, 4)])
        parts = []
        for g in range(FLD):
            total = rolled[0][(0 - g) % 4]
            for j in range(1, 4):
                total = jnp.where(block == j, rolled[j][(j - g) % 4], total)
            parts.append(total)
        gathered.append(jnp.concatenate(parts, axis=0))
    modes_at = dot_split(to_all, jnp.concatenate(gathered, axis=1)).astype(BF16)

    sums = []
    for p in range(PAIRS):
        modes = dot(modes_at[:, 128 * p : 128 * (p + 1)], leg4_ref[p])
        damped = (modes * inv_ref[p]).astype(BF16)
        damp_ref[p, 0:40, :] = damped
        sums.append(dot_nt(damped, leg4_ref[p]))

    returned = dot_split(back_all, jnp.concatenate(sums, axis=1))
    turned[...] = jnp.zeros_like(turned)
    for p in range(PAIRS):
        rolled = []
        for g in range(FLD):
            source = returned[16 * g : 16 * (g + 1), 128 * p : 128 * (p + 1)]
            rolled.append([source] + [pltpu.roll(source, 32 * k, 1) for k in range(1, 4)])
        for j in range(4):
            total = rolled[0][(0 - j) % 4]
            for g in range(1, 4):
                total = jnp.where(block == g, rolled[g][(g - j) % 4], total)
            at = 10 * (2 * p + (j >> 1)) + (j & 1)
            for c in range(2):
                turned[c, pl.ds(at, 8, stride=2), :] = total[8 * c : 8 * (c + 1)]
    for c in range(2):
        send2[:, c, :] = turned[c].T
    exchange(send2, recv2, 2, by_owner(lat, fld), by_group)

    for p in range(PAIRS):
        spec = dot(back_two, damp_ref[p, 0:40, :])
        spec = spec[0:40] + spec[40:80]
        for g in range(ALL_FIELDS):
            spec_ref[g, p, :, :] = spec[2 * g : 2 * g + 2, 0:PLACES]

    finish(recv2, 3)

    for c in range(2):
        turned[c] = recv2[:, c, :].T
    weight = keep * jnp.where(waves == 0.0, 1.0, 2.0)
    re, im = (
        jnp.concatenate([turned[c, 10 * s : 10 * s + 16, :] for s in range(SLOTS)], axis=1) * weight for c in range(2)
    )
    for b in range(4):
        tre_ref[16 * b : 16 * (b + 1), :] = re.astype(BF16)
        tim_ref[16 * b : 16 * (b + 1), :] = im.astype(BF16)
        if b < 3:
            re, im = re * zc - im * zs, re * zs + im * zc
    finish(send1, 0)
    finish(send2, 2)


def points_kernel(
    spec_in, cos_tab, sin_tab, tre_ref, tim_ref, size_ref, sel_ref, spec_out, out_ref, size_smem, sems
):
    move = pltpu.make_async_copy(spec_in, spec_out, sems.at[0])
    move.start()
    size = pltpu.make_async_copy(size_ref, size_smem, sems.at[1])
    size.start()
    flip = jnp.where(iota((128, 128), 0) + iota((128, 128), 1) == 127, 1.0, 0.0).astype(BF16)
    even = dot_nt(tre_ref[...], cos_tab[...])
    odd = dot_nt(tim_ref[...], sin_tab[...])
    size.wait()
    length = size_smem[0, 0]
    scale = 1.0 / jnp.sqrt(jnp.full((1, HALF), length.astype(F32), F32))
    ahead = (even - odd) * scale
    behind = ((even + odd) * scale).astype(BF16)
    behind = jnp.concatenate([behind, jnp.zeros((64, 768 - HALF), BF16)], axis=1)
    behind = dot(jnp.concatenate([behind[:, 128 * k : 128 * (k + 1)] for k in range(6)], axis=0), flip)
    behind = jnp.concatenate(
        [jnp.zeros((64, LANES - 768), F32)] + [behind[64 * k : 64 * (k + 1)] for k in range(5, -1, -1)], axis=1
    )
    behind = pltpu.roll(behind, length // 4 + 1, 1)
    ahead = jnp.concatenate([ahead, jnp.zeros((64, LANES - HALF), F32)], axis=1)
    across = iota((64, LANES), 1)
    total = jnp.where(across * 8 <= length, ahead, jnp.where(across * 4 < length, behind, 0.0)).astype(BF16)
    total = jnp.concatenate(
        [
            jnp.concatenate([total[16 * b : 16 * (b + 1), 128 * k : 128 * (k + 1)] for b in range(4)], axis=1)
            for k in range(CHUNKS)
        ],
        axis=0,
    )
    total = dot_nt(total, sel_ref[...])
    total = jnp.concatenate([total[16 * k : 16 * (k + 1)] for k in range(CHUNKS)], axis=1)[:, :WIDTH]
    for f in range(FIELDS):
        out_ref[f, :, :] = total[2 * f : 2 * f + 2].astype(BF16)
    move.wait()


def selection(flipped):
    column = iota((1, CHUNK), 1)
    across = column & 127
    target = (127 - across if flipped else across) * 4 + (column >> 7)
    return jnp.where(iota((CHUNK, CHUNK), 0) == target, 1.0, 0.0).astype(BF16)


def per_device(grid, row_lengths, band_map, fold_map, legendre, to_modes, back_modes, mode_rates):
    vmem = pl.BlockSpec(memory_space=pltpu.VMEM)
    anywhere = pl.BlockSpec(memory_space=pl.ANY)
    spec_shape = (ALL_FIELDS, PAIRS, 2, PLACES)
    held = pl.pallas_call(
        send_kernel,
        out_shape=(
            pltpu.VMEM(spec_shape, F32),
            pltpu.VMEM((HALF, WAVES), BF16),
            pltpu.VMEM((HALF, WAVES), BF16),
            pltpu.VMEM((64, WAVES), BF16),
            pltpu.VMEM((64, WAVES), BF16),
            pltpu.VMEM((8, 128), I32),
            pltpu.VMEM((CHUNK, CHUNK), BF16),
        ),
        in_specs=[pl.BlockSpec(memory_space=pltpu.HBM)] * 9,
        out_specs=(vmem,) * 7,
        scratch_shapes=[
            pltpu.SMEM((LAT,), I32),
            pltpu.SMEM((LAT,), I32),
            pltpu.SMEM((SLOTS, DEVS), I32),
            pltpu.VMEM((SLOTS, DEVS), I32),
            pltpu.VMEM((1, LAT), I32),
            pltpu.VMEM((FIELDS, 2, WIDTH), BF16),
            pltpu.VMEM((PAIRS, LAT, PLACES), F32),
            pltpu.VMEM((ALL_FIELDS, ALL_FIELDS), F32),
            pltpu.VMEM((ALL_FIELDS, ALL_FIELDS), F32),
            pltpu.VMEM((1, ALL_FIELDS), F32),
            pltpu.VMEM((48, WAVES), F32),
            pltpu.VMEM((48, WAVES), F32),
            pltpu.VMEM((CHUNK, CHUNK), BF16),
            pltpu.VMEM((PAIRS, 128, LANES), BF16),
            pltpu.VMEM((PAIRS, 40, LANES), F32),
            pltpu.VMEM((PAIRS, 48, LANES), BF16),
            pltpu.VMEM((64, WAVES), F32),
            pltpu.VMEM((64, WAVES), F32),
            pltpu.VMEM((2, 128, 128), F32),
            pltpu.VMEM((DEVS, 2, 128), F32),
            pltpu.VMEM((DEVS, 2, 128), F32),
            pltpu.VMEM((DEVS, 2, 128), F32),
            pltpu.VMEM((DEVS, 2, 128), F32),
            pltpu.SemaphoreType.DMA((10,)),
            pltpu.SemaphoreType.DMA((4,)),
        ],
        compiler_params=pltpu.CompilerParams(
            collective_id=0, has_side_effects=True, vmem_limit_bytes=24 * 1024 * 1024
        ),
        name="to_spectral",
    )(
        *[
            pltpu.with_memory_space_constraint(value, pltpu.HBM)
            for value in (
                row_lengths,
                band_map,
                fold_map.T,
                band_map.reshape(1, LAT),
                grid.reshape(FIELDS, 2, WIDTH),
                jnp.transpose(legendre, (0, 2, 1)),
                to_modes,
                back_modes,
                mode_rates.reshape(1, ALL_FIELDS),
            )
        ]
    )
    held = [pltpu.with_memory_space_constraint(value, pltpu.VMEM) for value in held]
    spectral, grid_out = pl.pallas_call(
        points_kernel,
        out_shape=(
            jax.ShapeDtypeStruct(spec_shape, F32),
            jax.ShapeDtypeStruct((FIELDS, 2, WIDTH), BF16),
        ),
        in_specs=[vmem] * 7,
        out_specs=(anywhere, vmem),
        scratch_shapes=[pltpu.SMEM((8, 128), I32), pltpu.SemaphoreType.DMA((2,))],
        compiler_params=pltpu.CompilerParams(vmem_limit_bytes=24 * 1024 * 1024),
        name="to_points",
    )(*held)
    return jnp.transpose(spectral, (0, 2, 1, 3)), grid_out.reshape(FIELDS, 1, 2, WIDTH)


def solution(mesh):
    placed = (
        P("fld", "lat", None, None),
        P(),
        P(),
        P(),
        P(("lat", "fld"), None, None),
        P(),
        P(),
        P(),
    )
    return jax.shard_map(
        per_device,
        mesh=mesh,
        in_specs=placed,
        out_specs=(P(None, None, ("lat", "fld"), None), P("fld", "lat", None, None)),
        check_vma=False,
    )
```

```python
import math

import jax
import jax.numpy as jnp
from jax import lax
from jax.experimental import pallas as pl
from jax.experimental.pallas import tpu as pltpu
from jax.sharding import PartitionSpec as P

HIGH = lax.Precision.HIGHEST
MESH = pl.DeviceIdType.MESH
F32, BF16, I32 = jnp.float32, jnp.bfloat16, jnp.int32
NT = (((1,), (1,)), ((), ()))
TN = (((0,), (0,)), ((), ()))

LAT, FLD = 32, 4
DEVS = LAT * FLD
FIELDS = 5
ALL_FIELDS = FIELDS * FLD
SLOTS = 10
PAIRS = SLOTS // 2
PLACES = 1281
CUT = 1279
WIDTH = 5248
WAVES = DEVS * SLOTS
HALF = 672
GROUP = 256
ROWS = 40
MAIN = PLACES - 1
UNROLL = 42
STEP = 16
BLOCKS = HALF // STEP
LANES = 1408
CHUNK = 512
CHUNKS = 11


def iota(shape, dim):
    return lax.broadcasted_iota(I32, shape, dim)


def dot(a, b, precision=None):
    return jnp.dot(a, b, precision=precision, preferred_element_type=F32)


def dot_tn(a, b):
    return lax.dot_general(a, b, TN, preferred_element_type=F32)


def dot_nt(a, b):
    return lax.dot_general(a, b, NT, preferred_element_type=F32)


SIN_TERMS = [(-1) ** k * math.pi ** (2 * k + 1) / math.factorial(2 * k + 1) for k in range(6)]
COS_TERMS = [(-1) ** k * math.pi ** (2 * k) / math.factorial(2 * k) for k in range(7)]


def horner(terms, square):
    total = jnp.full_like(square, terms[-1])
    for term in terms[-2::-1]:
        total = total * square + term
    return total


def turn(product, period, inverse):
    rest = product - period * jnp.round(product * inverse)
    part = rest * inverse
    square = part * part
    half_sin = part * horner(SIN_TERMS, square)
    half_cos = horner(COS_TERMS, square)
    return 1.0 - 2.0 * half_sin * half_sin, 2.0 * half_sin * half_cos


def row_of(value):
    return jnp.concatenate([value[s : s + 1] for s in range(SLOTS)], axis=1)


def split(value):
    upper = value.astype(BF16)
    return upper, (value - upper.astype(F32)).astype(BF16)


def triple(left):
    upper, lower = split(left)
    return jnp.concatenate([upper, upper, lower], axis=1)


def dot_triple(left, right):
    upper, lower = split(right)
    return dot(left, jnp.concatenate([upper, lower, upper], axis=0))


def offsets():
    hops = (0, 1, 2, 1)
    steps = [(x, y, z, c) for y in range(4) for z in range(4) for c in range(2) for x in range(4)][1:]
    return sorted(steps, key=lambda step: -(hops[step[0]] + hops[step[1]] + hops[step[2]]))


def send_kernel(
    len_hbm, band_s_hbm, fold_hbm, band_hbm, grid_hbm, leg_hbm, to_hbm, back_hbm, rate_hbm,
    spec_ref, cos_tab, sin_tab, tre_ref, tim_ref, size_ref, sel_ref,
    len_ref, band_s_ref, fold_s_ref, fold_ref, band_ref, grid_ref, leg_ref, to_ref, back_ref, rate_ref,
    wc_ref, ws_ref, rev_ref, leg4_ref, inv_ref, damp_ref, acc_c, acc_s, turned,
    send1, recv1, send2, recv2, in_sems, sems,
):
    lat = lax.axis_index("lat")
    fld = lax.axis_index("fld")
    owner = lat * FLD + fld

    moves = [
        pltpu.make_async_copy(source, dest, in_sems.at[k])
        for k, (source, dest) in enumerate(
            (
                (len_hbm, len_ref), (band_s_hbm, band_s_ref), (fold_hbm, fold_ref), (grid_hbm, grid_ref),
                (fold_hbm, fold_s_ref), (band_hbm, band_ref), (to_hbm, to_ref), (back_hbm, back_ref),
                (rate_hbm, rate_ref), (leg_hbm, leg_ref),
            )
        )
    ]
    for move in moves:
        move.start()

    high, middle, core = lat // 8, lax.rem(lat // 2, 4), lax.rem(lat, 2)
    xs, ys, zs_, cs = (
        [at] + [lax.rem(at + k, size) for k in range(1, size)]
        for at, size in ((fld, 4), (high, 4), (middle, 4), (core, 2))
    )
    peers = [(ys[y] * 8 + zs_[z] * 2 + cs[c], xs[x]) for x, y, z, c in offsets()]

    barrier = pltpu.get_barrier_semaphore()
    for o_lat, o_fld in peers:
        pl.semaphore_signal(barrier, inc=1, device_id={"lat": o_lat, "fld": o_fld}, device_id_type=MESH)

    sel_ref[...] = selection(False)
    rev_ref[...] = selection(True)

    for move in moves[:4]:
        move.wait()
    length = len_ref[band_s_ref[lat]]
    waves = row_of(fold_ref[...].astype(F32))
    full = jnp.full((1, WAVES), length.astype(F32), F32)
    size_ref[...] = jnp.full((8, 128), length, I32)
    quarter = full * 0.25
    inv_quarter = 1.0 / quarter
    scale = 1.0 / jnp.sqrt(full)
    keep = jnp.where(waves * 2.0 < full, 1.0, 0.0)
    zc, zs = turn(waves, full, 1.0 / full)

    base_c, base_s = turn(iota((STEP, WAVES), 0).astype(F32) * waves, quarter, inv_quarter)
    for start in range(0, 48, 8):
        c, s = turn((iota((8, WAVES), 0) + start).astype(F32) * (waves * float(STEP)), quarter, inv_quarter)
        wc_ref[start : start + 8, :] = c
        ws_ref[start : start + 8, :] = s
    points = jnp.concatenate([grid_ref[f].astype(F32) for f in range(FIELDS)], axis=0)
    points = jnp.where(iota((2 * FIELDS, WIDTH), 1) < length, points, 0.0)
    points = jnp.concatenate([points, jnp.zeros((16 - 2 * FIELDS, WIDTH), F32)], axis=0).astype(BF16)
    points = jnp.concatenate([points, jnp.zeros((16, CHUNK * CHUNKS - WIDTH), BF16)], axis=1)
    points = jnp.concatenate([points[:, CHUNK * k : CHUNK * (k + 1)] for k in range(CHUNKS)], axis=0)

    def by_phase(values, order):
        return jnp.concatenate(
            [
                jnp.concatenate([values[16 * k : 16 * (k + 1), 128 * b : 128 * (b + 1)] for k in order], axis=1)
                for b in range(4)
            ],
            axis=0,
        )

    ahead = by_phase(dot(points, sel_ref[...]), range(6))[:, :HALF]
    behind = by_phase(dot(points, rev_ref[...]), range(CHUNKS - 1, -1, -1))
    behind = pltpu.roll(behind, length // 4 + 1, 1)[:, :HALF]
    twice = (iota((64, HALF), 1) * 8).astype(F32)
    whole = full[:, :HALF]
    share = jnp.where(twice < whole, 1.0, jnp.where(twice == whole, 0.5, 0.0))

    plus = ((ahead + behind) * share).astype(BF16)
    minus = ((ahead - behind) * share).astype(BF16)
    for start in range(0, WAVES, GROUP):
        lanes = slice(start, start + GROUP)
        bc, bs = base_c[:, lanes], base_s[:, lanes]

        def fill(j, carry):
            c, s = wc_ref[pl.ds(j, 1), lanes], ws_ref[pl.ds(j, 1), lanes]
            rows = pl.ds(pl.multiple_of(j * STEP, STEP), STEP)
            cos_tab[rows, lanes] = (bc * c - bs * s).astype(BF16)
            sin_tab[rows, lanes] = (bs * c + bc * s).astype(BF16)
            return carry

        lax.fori_loop(0, BLOCKS, fill, 0, unroll=UNROLL)
        acc_c[:, lanes] = dot(plus, cos_tab[:, lanes])
        acc_s[:, lanes] = dot(minus, sin_tab[:, lanes])
    re, im = acc_c[48:64, :], -acc_s[48:64, :]
    for b in (2, 1, 0):
        re, im = (
            re * zc + im * zs + acc_c[16 * b : 16 * (b + 1), :],
            im * zc - re * zs - acc_s[16 * b : 16 * (b + 1), :],
        )
    for c, part in enumerate((re, im)):
        part = part * (scale * keep)
        packed = jnp.concatenate(
            [part[0:10, 128 * s : 128 * (s + 1)] for s in range(SLOTS)] + [jnp.zeros((28, 128), F32)], axis=0
        )
        send1[:, c, :] = packed.T

    def exchange(source, dest, sem, row, row_at):
        for o_lat, o_fld in peers:
            pltpu.make_async_remote_copy(
                src_ref=source.at[row_at(o_lat, o_fld)],
                dst_ref=dest.at[row],
                send_sem=sems.at[sem],
                recv_sem=sems.at[sem + 1],
                device_id={"lat": o_lat, "fld": o_fld},
                device_id_type=MESH,
            ).start()
        dest[row] = source[row_at(lat, fld)]

    def finish(buffer, sem):
        some = buffer.at[pl.ds(0, DEVS - 1)]
        pltpu.make_async_copy(some, some, sems.at[sem]).wait()

    by_owner = lambda a, b: a * FLD + b
    by_group = lambda a, b: b * LAT + a
    pl.semaphore_wait(barrier, DEVS - 1)
    exchange(send1, recv1, 0, by_group(lat, fld), by_owner)

    for move in moves[4:]:
        move.wait()
    perm = jnp.where(iota((LAT, LAT), 0) == band_ref[...], 1.0, 0.0)
    rates = jnp.sum(
        jnp.where((iota((ROWS, ALL_FIELDS), 0) >> 1) == iota((ROWS, ALL_FIELDS), 1), rate_ref[...], 0.0),
        axis=1, keepdims=True,
    )
    place = iota((1, MAIN), 1)
    quad = iota((1, 128), 1) >> 5
    wide_perm = jnp.concatenate([perm] * 4, axis=1).astype(BF16)
    final = 1.0 / (1.0 + rates)
    edges = []
    inv_ref[ROWS * PAIRS :, :] = jnp.zeros((8, MAIN), F32)
    for p in range(PAIRS):
        first = fold_s_ref[2 * p, owner]
        value = dot_tn(perm.astype(BF16), leg_ref[p, :, 0:MAIN].astype(BF16))
        partner = place > CUT - first
        one = jnp.where(partner, 0.0, value)
        two = jnp.where(partner, value, 0.0)
        sign_one = jnp.where((place & 1) == 1, -1.0, 1.0)
        sign_two = jnp.where(((place + first) & 1) == 1, -1.0, 1.0)
        for k, masked in enumerate((one, one * sign_one, two, two * sign_two)):
            leg4_ref[128 * p + 32 * k : 128 * p + 32 * (k + 1), :] = masked.astype(BF16)
        degree = jnp.where(partner, place - 1, first + place).astype(F32)
        tau = degree * (degree + 1.0) * (1.0 / float(CUT * (CUT + 1)))
        inv_ref[ROWS * p : ROWS * (p + 1), :] = 1.0 / (1.0 + rates * tau)
        edge = dot_tn(leg_ref[p, :, MAIN:PLACES].astype(BF16), wide_perm)
        odd = ((iota((1, 128), 1) * 0 + MAIN + first) & 1) == 1
        edges.append(jnp.where(quad < 2, 0.0, jnp.where((quad == 3) & odd, -edge, edge)))

    rows, cols = iota((ROWS, 64), 0), iota((ROWS, 64), 1)
    pick = jnp.where((iota((ROWS, 20), 0) >> 1) == iota((ROWS, 20), 1), 1.0, 0.0)
    spread_col = iota((20, 64), 1)
    spread = jnp.where(
        ((spread_col & 7) < FIELDS) & (iota((20, 64), 0) == (spread_col >> 4) * FIELDS + (spread_col & 7)), 1.0, 0.0
    )
    to_all = dot(dot(pick, to_ref[...], HIGH), spread, HIGH)
    to_all = triple(jnp.where((rows & 1) == ((cols >> 3) & 1), to_all, 0.0))
    pick_t = jnp.where(iota((20, ROWS), 0) == (iota((20, ROWS), 1) >> 1), 1.0, 0.0)
    half = dot(back_ref[...], pick_t, HIGH)
    back_rows = dot(pick, half, HIGH)
    back_rows = jnp.where((iota((ROWS, ROWS), 0) & 1) == (iota((ROWS, ROWS), 1) & 1), back_rows, 0.0)
    blank = jnp.zeros((ROWS, ROWS), F32)
    back_pair = jnp.concatenate(
        [jnp.concatenate([back_rows, blank], axis=1), jnp.concatenate([blank, back_rows], axis=1)], axis=0
    )
    back_pair = jnp.concatenate(split(back_pair), axis=0)

    spread_row = iota((64, 20), 0)
    spread_t = jnp.where(
        ((spread_row & 7) < FIELDS) & (iota((64, 20), 1) == (spread_row >> 4) * FIELDS + (spread_row & 7)), 1.0, 0.0
    )
    back_all = dot(spread_t, half, HIGH)
    back_all = jnp.where(((iota((64, ROWS), 0) >> 3) & 1) == (iota((64, ROWS), 1) & 1), back_all, 0.0)
    back_all = triple(back_all)

    finish(recv1, 1)

    for c in range(2):
        turned[c] = recv1[:, c, :].T
    block = iota((16, 128), 1) >> 5
    gathered = []
    for p in range(PAIRS):
        rolled = []
        for j in range(4):
            at = 10 * (2 * p + (j >> 1)) + (j & 1)
            source = jnp.concatenate([turned[c, pl.ds(at, 8, stride=2), :] for c in range(2)], axis=0)
            rolled.append([source] + [pltpu.roll(source, 32 * k, 1) for k in range(1, 4)])
        parts = []
        for g in range(FLD):
            total = rolled[0][(0 - g) % 4]
            for j in range(1, 4):
                total = jnp.where(block == j, rolled[j][(j - g) % 4], total)
            parts.append(total)
        gathered.append(jnp.concatenate(parts, axis=0))
    modes_at = dot_triple(to_all, jnp.concatenate(gathered, axis=1))
    nothing = jnp.zeros((ROWS, 128), F32)
    sums, ends = [], []
    for p in range(0, PAIRS, 2):
        at = [modes_at[:, 128 * q : 128 * (q + 1)] if q < PAIRS else nothing for q in (p, p + 1)]
        both = jnp.concatenate(
            [jnp.concatenate([at[0], nothing], axis=1), jnp.concatenate([nothing, at[1]], axis=1)], axis=0
        ).astype(BF16)
        if p + 1 == PAIRS:
            both = both[0:48, 0:128]
        count = both.shape[0]
        tables = slice(128 * p, 128 * p + both.shape[1])
        places = inv_ref[ROWS * p : ROWS * p + count, :]
        damped = (dot(both, leg4_ref[tables, :]) * places).astype(BF16)
        damp_ref[p // 2, 0:count, :] = damped
        total = dot_nt(damped, leg4_ref[tables, :])
        for k in range(min(2, PAIRS - p)):
            exact = at[k].astype(BF16).astype(F32)
            end = jnp.sum(exact * edges[p + k], axis=1, keepdims=True) * final
            ends.append(end)
            sums.append(total[ROWS * k : ROWS * (k + 1), 128 * k : 128 * (k + 1)] + end * edges[p + k])

    returned = dot_triple(back_all, jnp.concatenate(sums, axis=1))
    turned[...] = jnp.zeros_like(turned)
    for p in range(PAIRS):
        rolled = []
        for g in range(FLD):
            source = returned[16 * g : 16 * (g + 1), 128 * p : 128 * (p + 1)]
            rolled.append([source] + [pltpu.roll(source, 32 * k, 1) for k in range(1, 4)])
        for j in range(4):
            total = rolled[0][(0 - j) % 4]
            for g in range(1, 4):
                total = jnp.where(block == g, rolled[g][(g - j) % 4], total)
            at = 10 * (2 * p + (j >> 1)) + (j & 1)
            for c in range(2):
                turned[c, pl.ds(at, 8, stride=2), :] = total[8 * c : 8 * (c + 1)]
    for c in range(2):
        send2[:, c, :] = turned[c].T
    exchange(send2, recv2, 2, by_owner(lat, fld), by_group)

    lane = iota((ROWS, 128), 1)
    last = jnp.zeros((ROWS, 128), F32)
    for p in range(PAIRS):
        last = jnp.where(lane == p, ends[p], last)
    last = dot(back_rows, last, HIGH)
    for p in range(0, PAIRS, 2):
        count = 2 if p + 1 < PAIRS else 1
        depth = 2 * ROWS if count == 2 else 48
        spec = dot(back_pair[:, 0:depth], damp_ref[p // 2, 0:depth, :])
        spec = spec[0 : 2 * ROWS] + spec[2 * ROWS : 4 * ROWS]
        for k in range(count):
            block_rows = jnp.concatenate(
                [spec[ROWS * k : ROWS * (k + 1)], last[:, p + k : p + k + 1]], axis=1
            )
            for g in range(ALL_FIELDS):
                spec_ref[g, p + k, :, :] = block_rows[2 * g : 2 * g + 2]

    finish(recv2, 3)

    for c in range(2):
        turned[c] = recv2[:, c, :].T
    weight = keep * jnp.where(waves == 0.0, 1.0, 2.0)
    re, im = (
        jnp.concatenate([turned[c, 10 * s : 10 * s + 16, :] for s in range(SLOTS)], axis=1) * weight for c in range(2)
    )
    for b in range(4):
        tre_ref[16 * b : 16 * (b + 1), :] = re.astype(BF16)
        tim_ref[16 * b : 16 * (b + 1), :] = im.astype(BF16)
        if b < 3:
            re, im = re * zc - im * zs, re * zs + im * zc
    finish(send1, 0)
    finish(send2, 2)


def points_kernel(
    spec_in, cos_tab, sin_tab, tre_ref, tim_ref, size_ref, sel_ref, spec_out, out_ref, size_smem, sems
):
    move = pltpu.make_async_copy(spec_in, spec_out, sems.at[0])
    move.start()
    size = pltpu.make_async_copy(size_ref, size_smem, sems.at[1])
    size.start()
    flip = jnp.where(iota((128, 128), 0) + iota((128, 128), 1) == 127, 1.0, 0.0).astype(BF16)
    even = dot_nt(tre_ref[...], cos_tab[...])
    odd = dot_nt(tim_ref[...], sin_tab[...])
    size.wait()
    length = size_smem[0, 0]
    scale = 1.0 / jnp.sqrt(jnp.full((1, HALF), length.astype(F32), F32))
    ahead = (even - odd) * scale
    behind = ((even + odd) * scale).astype(BF16)
    behind = jnp.concatenate([behind, jnp.zeros((64, 768 - HALF), BF16)], axis=1)
    behind = dot(jnp.concatenate([behind[:, 128 * k : 128 * (k + 1)] for k in range(6)], axis=0), flip)
    behind = jnp.concatenate(
        [jnp.zeros((64, LANES - 768), F32)] + [behind[64 * k : 64 * (k + 1)] for k in range(5, -1, -1)], axis=1
    )
    behind = pltpu.roll(behind, length // 4 + 1, 1)
    ahead = jnp.concatenate([ahead, jnp.zeros((64, LANES - HALF), F32)], axis=1)
    across = iota((64, LANES), 1)
    total = jnp.where(across * 8 <= length, ahead, jnp.where(across * 4 < length, behind, 0.0)).astype(BF16)
    total = jnp.concatenate(
        [
            jnp.concatenate([total[16 * b : 16 * (b + 1), 128 * k : 128 * (k + 1)] for b in range(4)], axis=1)
            for k in range(CHUNKS)
        ],
        axis=0,
    )
    total = dot_nt(total, sel_ref[...])
    total = jnp.concatenate([total[16 * k : 16 * (k + 1)] for k in range(CHUNKS)], axis=1)[:, :WIDTH]
    for f in range(FIELDS):
        out_ref[f, :, :] = total[2 * f : 2 * f + 2].astype(BF16)
    move.wait()


def selection(flipped):
    column = iota((1, CHUNK), 1)
    across = column & 127
    target = (127 - across if flipped else across) * 4 + (column >> 7)
    return jnp.where(iota((CHUNK, CHUNK), 0) == target, 1.0, 0.0).astype(BF16)


def per_device(grid, row_lengths, band_map, fold_map, legendre, to_modes, back_modes, mode_rates):
    vmem = pl.BlockSpec(memory_space=pltpu.VMEM)
    anywhere = pl.BlockSpec(memory_space=pl.ANY)
    spec_shape = (ALL_FIELDS, PAIRS, 2, PLACES)
    held = pl.pallas_call(
        send_kernel,
        out_shape=(
            pltpu.VMEM(spec_shape, F32),
            pltpu.VMEM((HALF, WAVES), BF16),
            pltpu.VMEM((HALF, WAVES), BF16),
            pltpu.VMEM((64, WAVES), BF16),
            pltpu.VMEM((64, WAVES), BF16),
            pltpu.VMEM((8, 128), I32),
            pltpu.VMEM((CHUNK, CHUNK), BF16),
        ),
        in_specs=[pl.BlockSpec(memory_space=pltpu.HBM)] * 9,
        out_specs=(vmem,) * 7,
        scratch_shapes=[
            pltpu.SMEM((LAT,), I32),
            pltpu.SMEM((LAT,), I32),
            pltpu.SMEM((SLOTS, DEVS), I32),
            pltpu.VMEM((SLOTS, DEVS), I32),
            pltpu.VMEM((1, LAT), I32),
            pltpu.VMEM((FIELDS, 2, WIDTH), BF16),
            pltpu.VMEM((PAIRS, LAT, PLACES), F32),
            pltpu.VMEM((ALL_FIELDS, ALL_FIELDS), F32),
            pltpu.VMEM((ALL_FIELDS, ALL_FIELDS), F32),
            pltpu.VMEM((1, ALL_FIELDS), F32),
            pltpu.VMEM((48, WAVES), F32),
            pltpu.VMEM((48, WAVES), F32),
            pltpu.VMEM((CHUNK, CHUNK), BF16),
            pltpu.VMEM((PAIRS * 128, MAIN), BF16),
            pltpu.VMEM((PAIRS * ROWS + 8, MAIN), F32),
            pltpu.VMEM(((PAIRS + 1) // 2, 2 * ROWS, MAIN), BF16),
            pltpu.VMEM((64, WAVES), F32),
            pltpu.VMEM((64, WAVES), F32),
            pltpu.VMEM((2, 128, 128), F32),
            pltpu.VMEM((DEVS, 2, 128), F32),
            pltpu.VMEM((DEVS, 2, 128), F32),
            pltpu.VMEM((DEVS, 2, 128), F32),
            pltpu.VMEM((DEVS, 2, 128), F32),
            pltpu.SemaphoreType.DMA((10,)),
            pltpu.SemaphoreType.DMA((4,)),
        ],
        compiler_params=pltpu.CompilerParams(
            collective_id=0, has_side_effects=True, vmem_limit_bytes=24 * 1024 * 1024
        ),
        name="to_spectral",
    )(
        *[
            pltpu.with_memory_space_constraint(value, pltpu.HBM)
            for value in (
                row_lengths,
                band_map,
                fold_map.T,
                band_map.reshape(1, LAT),
                grid.reshape(FIELDS, 2, WIDTH),
                jnp.transpose(legendre, (0, 2, 1)),
                to_modes,
                back_modes,
                mode_rates.reshape(1, ALL_FIELDS),
            )
        ]
    )
    held = [pltpu.with_memory_space_constraint(value, pltpu.VMEM) for value in held]
    spectral, grid_out = pl.pallas_call(
        points_kernel,
        out_shape=(
            jax.ShapeDtypeStruct(spec_shape, F32),
            jax.ShapeDtypeStruct((FIELDS, 2, WIDTH), BF16),
        ),
        in_specs=[vmem] * 7,
        out_specs=(anywhere, vmem),
        scratch_shapes=[pltpu.SMEM((8, 128), I32), pltpu.SemaphoreType.DMA((2,))],
        compiler_params=pltpu.CompilerParams(vmem_limit_bytes=24 * 1024 * 1024),
        name="to_points",
    )(*held)
    return jnp.transpose(spectral, (0, 2, 1, 3)), grid_out.reshape(FIELDS, 1, 2, WIDTH)


def solution(mesh):
    placed = (
        P("fld", "lat", None, None),
        P(),
        P(),
        P(),
        P(("lat", "fld"), None, None),
        P(),
        P(),
        P(),
    )
    return jax.shard_map(
        per_device,
        mesh=mesh,
        in_specs=placed,
        out_specs=(P(None, None, ("lat", "fld"), None), P("fld", "lat", None, None)),
        check_vma=False,
    )
```

```python
import math
import random

import jax
import jax.numpy as jnp
from jax import lax
from jax.experimental import pallas as pl
from jax.experimental.pallas import tpu as pltpu
from jax.sharding import PartitionSpec as P

HIGH = lax.Precision.HIGHEST
MESH = pl.DeviceIdType.MESH
F32, BF16, I32 = jnp.float32, jnp.bfloat16, jnp.int32
NT = (((1,), (1,)), ((), ()))
TN = (((0,), (0,)), ((), ()))

LAT, FLD = 32, 4
DEVS = LAT * FLD
FIELDS = 5
ALL_FIELDS = FIELDS * FLD
SLOTS = 10
PAIRS = SLOTS // 2
PLACES = 1281
CUT = 1279
WIDTH = 5248
WAVES = DEVS * SLOTS
HALF = 656
GROUP = 256
ROWS = 40
MAIN = PLACES - 1
UNROLL = 41
STEP = 16
BLOCKS = HALF // STEP
LANES = 1408
CHUNK = 512
CHUNKS = 11


def iota(shape, dim):
    return lax.broadcasted_iota(I32, shape, dim)


def dot(a, b, precision=None):
    return jnp.dot(a, b, precision=precision, preferred_element_type=F32)


def dot_tn(a, b):
    return lax.dot_general(a, b, TN, preferred_element_type=F32)


def dot_nt(a, b):
    return lax.dot_general(a, b, NT, preferred_element_type=F32)


SIN_TERMS = [(-1) ** k * math.pi ** (2 * k + 1) / math.factorial(2 * k + 1) for k in range(6)]
COS_TERMS = [(-1) ** k * math.pi ** (2 * k) / math.factorial(2 * k) for k in range(7)]


def horner(terms, square):
    total = jnp.full_like(square, terms[-1])
    for term in terms[-2::-1]:
        total = total * square + term
    return total


def turn(product, period, inverse):
    rest = product - period * jnp.round(product * inverse)
    part = rest * inverse
    square = part * part
    half_sin = part * horner(SIN_TERMS, square)
    half_cos = horner(COS_TERMS, square)
    return 1.0 - 2.0 * half_sin * half_sin, 2.0 * half_sin * half_cos


def row_of(value):
    return jnp.concatenate([value[s : s + 1] for s in range(SLOTS)], axis=1)


def split(value):
    upper = value.astype(BF16)
    return upper, (value - upper.astype(F32)).astype(BF16)


def triple(left):
    upper, lower = split(left)
    return jnp.concatenate([upper, upper, lower], axis=1)


def dot_triple(left, right):
    upper, lower = split(right)
    return dot(left, jnp.concatenate([upper, lower, upper], axis=0))


def offsets():
    hops = (0, 1, 2, 1)
    steps = [(x, y, z, c) for y in range(4) for z in range(4) for c in range(2) for x in range(4)][1:]
    random.Random(5).shuffle(steps)
    return sorted(steps, key=lambda step: -(hops[step[0]] + hops[step[1]] + hops[step[2]]))


def send_kernel(
    len_hbm, band_s_hbm, fold_hbm, band_hbm, grid_hbm, leg_hbm, to_hbm, back_hbm, rate_hbm,
    spec_ref, cos_tab, sin_tab, tre_ref, tim_ref, size_ref, sel_ref,
    len_ref, band_s_ref, fold_s_ref, fold_ref, band_ref, grid_ref, leg_ref, to_ref, back_ref, rate_ref,
    wc_ref, ws_ref, rev_ref, leg4_ref, inv_ref, damp_ref, acc_c, acc_s, turned,
    send1, recv1, send2, recv2, in_sems, sems,
):
    lat = lax.axis_index("lat")
    fld = lax.axis_index("fld")
    owner = lat * FLD + fld

    moves = [
        pltpu.make_async_copy(source, dest, in_sems.at[k])
        for k, (source, dest) in enumerate(
            (
                (len_hbm, len_ref), (band_s_hbm, band_s_ref), (fold_hbm, fold_ref), (grid_hbm, grid_ref),
                (fold_hbm, fold_s_ref), (band_hbm, band_ref), (to_hbm, to_ref), (back_hbm, back_ref),
                (rate_hbm, rate_ref), (leg_hbm, leg_ref),
            )
        )
    ]
    for move in moves:
        move.start()

    high, middle, core = lat // 8, lax.rem(lat // 2, 4), lax.rem(lat, 2)
    xs, ys, zs_, cs = (
        [at] + [lax.rem(at + k, size) for k in range(1, size)]
        for at, size in ((fld, 4), (high, 4), (middle, 4), (core, 2))
    )
    peers = [(ys[y] * 8 + zs_[z] * 2 + cs[c], xs[x]) for x, y, z, c in offsets()]

    barrier = pltpu.get_barrier_semaphore()
    for o_lat, o_fld in peers:
        pl.semaphore_signal(barrier, inc=1, device_id={"lat": o_lat, "fld": o_fld}, device_id_type=MESH)

    sel_ref[...] = selection(False)
    rev_ref[...] = selection(True)

    for move in moves[:4]:
        move.wait()
    length = len_ref[band_s_ref[lat]]
    waves = row_of(fold_ref[...].astype(F32))
    full = jnp.full((1, WAVES), length.astype(F32), F32)
    size_ref[...] = jnp.full((8, 128), length, I32)
    quarter = full * 0.25
    inv_quarter = 1.0 / quarter
    scale = 1.0 / jnp.sqrt(full)
    keep = jnp.where(waves * 2.0 < full, 1.0, 0.0)
    zc, zs = turn(waves, full, 1.0 / full)

    base_c, base_s = turn(iota((STEP, WAVES), 0).astype(F32) * waves, quarter, inv_quarter)
    for start in range(0, 48, 8):
        c, s = turn((iota((8, WAVES), 0) + start).astype(F32) * (waves * float(STEP)), quarter, inv_quarter)
        wc_ref[start : start + 8, :] = c
        ws_ref[start : start + 8, :] = s
    points = jnp.concatenate([grid_ref[f].astype(F32) for f in range(FIELDS)], axis=0)
    points = jnp.where(iota((2 * FIELDS, WIDTH), 1) < length, points, 0.0)
    points = jnp.concatenate([points, jnp.zeros((16 - 2 * FIELDS, WIDTH), F32)], axis=0).astype(BF16)
    points = jnp.concatenate([points, jnp.zeros((16, CHUNK * CHUNKS - WIDTH), BF16)], axis=1)
    points = jnp.concatenate([points[:, CHUNK * k : CHUNK * (k + 1)] for k in range(CHUNKS)], axis=0)

    def by_phase(values, order):
        return jnp.concatenate(
            [
                jnp.concatenate([values[16 * k : 16 * (k + 1), 128 * b : 128 * (b + 1)] for k in order], axis=1)
                for b in range(4)
            ],
            axis=0,
        )

    ahead = by_phase(dot(points, sel_ref[...]), range(6))[:, :HALF]
    behind = by_phase(dot(points, rev_ref[...]), range(CHUNKS - 1, -1, -1))
    behind = pltpu.roll(behind, length // 4 + 1, 1)[:, :HALF]
    twice = (iota((64, HALF), 1) * 8).astype(F32)
    whole = full[:, :HALF]
    share = jnp.where(twice < whole, 1.0, jnp.where(twice == whole, 0.5, 0.0))

    plus = ((ahead + behind) * share).astype(BF16)
    minus = ((ahead - behind) * share).astype(BF16)
    for start in range(0, WAVES, GROUP):
        lanes = slice(start, start + GROUP)
        bc, bs = base_c[:, lanes], base_s[:, lanes]

        def fill(j, carry):
            c, s = wc_ref[pl.ds(j, 1), lanes], ws_ref[pl.ds(j, 1), lanes]
            rows = pl.ds(pl.multiple_of(j * STEP, STEP), STEP)
            cos_tab[rows, lanes] = (bc * c - bs * s).astype(BF16)
            sin_tab[rows, lanes] = (bs * c + bc * s).astype(BF16)
            return carry

        lax.fori_loop(0, BLOCKS, fill, 0, unroll=UNROLL)
        acc_c[:, lanes] = dot(plus, cos_tab[:, lanes])
        acc_s[:, lanes] = dot(minus, sin_tab[:, lanes])
    re, im = acc_c[48:64, :], -acc_s[48:64, :]
    for b in (2, 1, 0):
        re, im = (
            re * zc + im * zs + acc_c[16 * b : 16 * (b + 1), :],
            im * zc - re * zs - acc_s[16 * b : 16 * (b + 1), :],
        )
    for c, part in enumerate((re, im)):
        part = part * (scale * keep)
        packed = jnp.concatenate(
            [part[0:10, 128 * s : 128 * (s + 1)] for s in range(SLOTS)] + [jnp.zeros((28, 128), F32)], axis=0
        )
        send1[:, c, :] = packed.T

    def exchange(source, dest, sem, row, row_at):
        for o_lat, o_fld in peers:
            pltpu.make_async_remote_copy(
                src_ref=source.at[row_at(o_lat, o_fld)],
                dst_ref=dest.at[row],
                send_sem=sems.at[sem],
                recv_sem=sems.at[sem + 1],
                device_id={"lat": o_lat, "fld": o_fld},
                device_id_type=MESH,
            ).start()
        dest[row] = source[row_at(lat, fld)]

    def finish(buffer, sem):
        some = buffer.at[pl.ds(0, DEVS - 1)]
        pltpu.make_async_copy(some, some, sems.at[sem]).wait()

    by_owner = lambda a, b: a * FLD + b
    by_group = lambda a, b: b * LAT + a
    pl.semaphore_wait(barrier, DEVS - 1)
    exchange(send1, recv1, 0, by_group(lat, fld), by_owner)

    for move in moves[4:]:
        move.wait()
    perm = jnp.where(iota((LAT, LAT), 0) == band_ref[...], 1.0, 0.0)
    rates = jnp.sum(
        jnp.where((iota((ROWS, ALL_FIELDS), 0) >> 1) == iota((ROWS, ALL_FIELDS), 1), rate_ref[...], 0.0),
        axis=1, keepdims=True,
    )
    place = iota((1, MAIN), 1)
    quad = iota((1, 128), 1) >> 5
    wide_perm = jnp.concatenate([perm] * 4, axis=1).astype(BF16)
    final = 1.0 / (1.0 + rates)
    edges = []
    inv_ref[ROWS * PAIRS :, :] = jnp.zeros((8, MAIN), F32)
    for p in range(PAIRS):
        first = fold_s_ref[2 * p, owner]
        value = dot_tn(perm.astype(BF16), leg_ref[p, :, 0:MAIN].astype(BF16))
        partner = place > CUT - first
        one = jnp.where(partner, 0.0, value)
        two = jnp.where(partner, value, 0.0)
        sign_one = jnp.where((place & 1) == 1, -1.0, 1.0)
        sign_two = jnp.where(((place + first) & 1) == 1, -1.0, 1.0)
        for k, masked in enumerate((one, one * sign_one, two, two * sign_two)):
            leg4_ref[128 * p + 32 * k : 128 * p + 32 * (k + 1), :] = masked.astype(BF16)
        degree = jnp.where(partner, place - 1, first + place).astype(F32)
        tau = degree * (degree + 1.0) * (1.0 / float(CUT * (CUT + 1)))
        inv_ref[ROWS * p : ROWS * (p + 1), :] = 1.0 / (1.0 + rates * tau)
        edge = dot_tn(leg_ref[p, :, MAIN:PLACES].astype(BF16), wide_perm)
        odd = ((iota((1, 128), 1) * 0 + MAIN + first) & 1) == 1
        edges.append(jnp.where(quad < 2, 0.0, jnp.where((quad == 3) & odd, -edge, edge)))

    rows, cols = iota((ROWS, 64), 0), iota((ROWS, 64), 1)
    pick = jnp.where((iota((ROWS, 20), 0) >> 1) == iota((ROWS, 20), 1), 1.0, 0.0)
    spread_col = iota((20, 64), 1)
    spread = jnp.where(
        ((spread_col & 7) < FIELDS) & (iota((20, 64), 0) == (spread_col >> 4) * FIELDS + (spread_col & 7)), 1.0, 0.0
    )
    to_all = dot(dot(pick, to_ref[...], HIGH), spread, HIGH)
    to_all = triple(jnp.where((rows & 1) == ((cols >> 3) & 1), to_all, 0.0))
    pick_t = jnp.where(iota((20, ROWS), 0) == (iota((20, ROWS), 1) >> 1), 1.0, 0.0)
    half = dot(back_ref[...], pick_t, HIGH)
    back_rows = dot(pick, half, HIGH)
    back_rows = jnp.where((iota((ROWS, ROWS), 0) & 1) == (iota((ROWS, ROWS), 1) & 1), back_rows, 0.0)
    blank = jnp.zeros((ROWS, ROWS), F32)
    back_pair = jnp.concatenate(
        [jnp.concatenate([back_rows, blank], axis=1), jnp.concatenate([blank, back_rows], axis=1)], axis=0
    )
    back_pair = jnp.concatenate(split(back_pair), axis=0)

    spread_row = iota((64, 20), 0)
    spread_t = jnp.where(
        ((spread_row & 7) < FIELDS) & (iota((64, 20), 1) == (spread_row >> 4) * FIELDS + (spread_row & 7)), 1.0, 0.0
    )
    back_all = dot(spread_t, half, HIGH)
    back_all = jnp.where(((iota((64, ROWS), 0) >> 3) & 1) == (iota((64, ROWS), 1) & 1), back_all, 0.0)
    back_all = triple(back_all)

    finish(recv1, 1)

    for c in range(2):
        turned[c] = recv1[:, c, :].T
    block = iota((16, 128), 1) >> 5
    gathered = []
    for p in range(PAIRS):
        rolled = []
        for j in range(4):
            at = 10 * (2 * p + (j >> 1)) + (j & 1)
            source = jnp.concatenate([turned[c, pl.ds(at, 8, stride=2), :] for c in range(2)], axis=0)
            rolled.append([source] + [pltpu.roll(source, 32 * k, 1) for k in range(1, 4)])
        parts = []
        for g in range(FLD):
            total = rolled[0][(0 - g) % 4]
            for j in range(1, 4):
                total = jnp.where(block == j, rolled[j][(j - g) % 4], total)
            parts.append(total)
        gathered.append(jnp.concatenate(parts, axis=0))
    modes_at = dot_triple(to_all, jnp.concatenate(gathered, axis=1))
    nothing = jnp.zeros((ROWS, 128), F32)
    sums, ends = [], []
    for p in range(0, PAIRS, 2):
        at = [modes_at[:, 128 * q : 128 * (q + 1)] if q < PAIRS else nothing for q in (p, p + 1)]
        both = jnp.concatenate(
            [jnp.concatenate([at[0], nothing], axis=1), jnp.concatenate([nothing, at[1]], axis=1)], axis=0
        ).astype(BF16)
        if p + 1 == PAIRS:
            both = both[0:48, 0:128]
        count = both.shape[0]
        tables = slice(128 * p, 128 * p + both.shape[1])
        places = inv_ref[ROWS * p : ROWS * p + count, :]
        damped = (dot(both, leg4_ref[tables, :]) * places).astype(BF16)
        damp_ref[p // 2, 0:count, :] = damped
        total = dot_nt(damped, leg4_ref[tables, :])
        for k in range(min(2, PAIRS - p)):
            exact = at[k].astype(BF16).astype(F32)
            end = jnp.sum(exact * edges[p + k], axis=1, keepdims=True) * final
            ends.append(end)
            sums.append(total[ROWS * k : ROWS * (k + 1), 128 * k : 128 * (k + 1)] + end * edges[p + k])

    returned = dot_triple(back_all, jnp.concatenate(sums, axis=1))
    turned[...] = jnp.zeros_like(turned)
    for p in range(PAIRS):
        rolled = []
        for g in range(FLD):
            source = returned[16 * g : 16 * (g + 1), 128 * p : 128 * (p + 1)]
            rolled.append([source] + [pltpu.roll(source, 32 * k, 1) for k in range(1, 4)])
        for j in range(4):
            total = rolled[0][(0 - j) % 4]
            for g in range(1, 4):
                total = jnp.where(block == g, rolled[g][(g - j) % 4], total)
            at = 10 * (2 * p + (j >> 1)) + (j & 1)
            for c in range(2):
                turned[c, pl.ds(at, 8, stride=2), :] = total[8 * c : 8 * (c + 1)]
    for c in range(2):
        send2[:, c, :] = turned[c].T
    exchange(send2, recv2, 2, by_owner(lat, fld), by_group)

    lane = iota((ROWS, 128), 1)
    last = jnp.zeros((ROWS, 128), F32)
    for p in range(PAIRS):
        last = jnp.where(lane == p, ends[p], last)
    last = dot(back_rows, last, HIGH)
    for p in range(0, PAIRS, 2):
        count = 2 if p + 1 < PAIRS else 1
        depth = 2 * ROWS if count == 2 else 48
        spec = dot(back_pair[:, 0:depth], damp_ref[p // 2, 0:depth, :])
        spec = spec[0 : 2 * ROWS] + spec[2 * ROWS : 4 * ROWS]
        for k in range(count):
            block_rows = jnp.concatenate(
                [spec[ROWS * k : ROWS * (k + 1)], last[:, p + k : p + k + 1]], axis=1
            )
            for g in range(ALL_FIELDS):
                spec_ref[g, p + k, :, :] = block_rows[2 * g : 2 * g + 2]

    finish(recv2, 3)

    for c in range(2):
        turned[c] = recv2[:, c, :].T
    weight = keep * jnp.where(waves == 0.0, 1.0, 2.0)
    re, im = (
        jnp.concatenate([turned[c, 10 * s : 10 * s + 16, :] for s in range(SLOTS)], axis=1) * weight for c in range(2)
    )
    for b in range(4):
        tre_ref[16 * b : 16 * (b + 1), :] = re.astype(BF16)
        tim_ref[16 * b : 16 * (b + 1), :] = im.astype(BF16)
        if b < 3:
            re, im = re * zc - im * zs, re * zs + im * zc
    finish(send1, 0)
    finish(send2, 2)


def points_kernel(
    spec_in, cos_tab, sin_tab, tre_ref, tim_ref, size_ref, sel_ref, spec_out, out_ref, size_smem, sems
):
    move = pltpu.make_async_copy(spec_in, spec_out, sems.at[0])
    move.start()
    size = pltpu.make_async_copy(size_ref, size_smem, sems.at[1])
    size.start()
    flip = jnp.where(iota((128, 128), 0) + iota((128, 128), 1) == 127, 1.0, 0.0).astype(BF16)
    even = dot_nt(tre_ref[...], cos_tab[...])
    odd = dot_nt(tim_ref[...], sin_tab[...])
    size.wait()
    length = size_smem[0, 0]
    scale = 1.0 / jnp.sqrt(jnp.full((1, HALF), length.astype(F32), F32))
    ahead = (even - odd) * scale
    behind = ((even + odd) * scale).astype(BF16)
    behind = jnp.concatenate([behind, jnp.zeros((64, 768 - HALF), BF16)], axis=1)
    behind = dot(jnp.concatenate([behind[:, 128 * k : 128 * (k + 1)] for k in range(6)], axis=0), flip)
    behind = jnp.concatenate(
        [jnp.zeros((64, LANES - 768), F32)] + [behind[64 * k : 64 * (k + 1)] for k in range(5, -1, -1)], axis=1
    )
    behind = pltpu.roll(behind, length // 4 + 1, 1)
    ahead = jnp.concatenate([ahead, jnp.zeros((64, LANES - HALF), F32)], axis=1)
    across = iota((64, LANES), 1)
    total = jnp.where(across * 8 <= length, ahead, jnp.where(across * 4 < length, behind, 0.0)).astype(BF16)
    total = jnp.concatenate(
        [
            jnp.concatenate([total[16 * b : 16 * (b + 1), 128 * k : 128 * (k + 1)] for b in range(4)], axis=1)
            for k in range(CHUNKS)
        ],
        axis=0,
    )
    total = dot_nt(total, sel_ref[...])
    total = jnp.concatenate([total[16 * k : 16 * (k + 1)] for k in range(CHUNKS)], axis=1)[:, :WIDTH]
    for f in range(FIELDS):
        out_ref[f, :, :] = total[2 * f : 2 * f + 2].astype(BF16)
    move.wait()


def selection(flipped):
    column = iota((1, CHUNK), 1)
    across = column & 127
    target = (127 - across if flipped else across) * 4 + (column >> 7)
    return jnp.where(iota((CHUNK, CHUNK), 0) == target, 1.0, 0.0).astype(BF16)


def per_device(grid, row_lengths, band_map, fold_map, legendre, to_modes, back_modes, mode_rates):
    vmem = pl.BlockSpec(memory_space=pltpu.VMEM)
    anywhere = pl.BlockSpec(memory_space=pl.ANY)
    spec_shape = (ALL_FIELDS, PAIRS, 2, PLACES)
    held = pl.pallas_call(
        send_kernel,
        out_shape=(
            pltpu.VMEM(spec_shape, F32),
            pltpu.VMEM((HALF, WAVES), BF16),
            pltpu.VMEM((HALF, WAVES), BF16),
            pltpu.VMEM((64, WAVES), BF16),
            pltpu.VMEM((64, WAVES), BF16),
            pltpu.VMEM((8, 128), I32),
            pltpu.VMEM((CHUNK, CHUNK), BF16),
        ),
        in_specs=[pl.BlockSpec(memory_space=pltpu.HBM)] * 9,
        out_specs=(vmem,) * 7,
        scratch_shapes=[
            pltpu.SMEM((LAT,), I32),
            pltpu.SMEM((LAT,), I32),
            pltpu.SMEM((SLOTS, DEVS), I32),
            pltpu.VMEM((SLOTS, DEVS), I32),
            pltpu.VMEM((1, LAT), I32),
            pltpu.VMEM((FIELDS, 2, WIDTH), BF16),
            pltpu.VMEM((PAIRS, LAT, PLACES), F32),
            pltpu.VMEM((ALL_FIELDS, ALL_FIELDS), F32),
            pltpu.VMEM((ALL_FIELDS, ALL_FIELDS), F32),
            pltpu.VMEM((1, ALL_FIELDS), F32),
            pltpu.VMEM((48, WAVES), F32),
            pltpu.VMEM((48, WAVES), F32),
            pltpu.VMEM((CHUNK, CHUNK), BF16),
            pltpu.VMEM((PAIRS * 128, MAIN), BF16),
            pltpu.VMEM((PAIRS * ROWS + 8, MAIN), F32),
            pltpu.VMEM(((PAIRS + 1) // 2, 2 * ROWS, MAIN), BF16),
            pltpu.VMEM((64, WAVES), F32),
            pltpu.VMEM((64, WAVES), F32),
            pltpu.VMEM((2, 128, 128), F32),
            pltpu.VMEM((DEVS, 2, 128), F32),
            pltpu.VMEM((DEVS, 2, 128), F32),
            pltpu.VMEM((DEVS, 2, 128), F32),
            pltpu.VMEM((DEVS, 2, 128), F32),
            pltpu.SemaphoreType.DMA((10,)),
            pltpu.SemaphoreType.DMA((4,)),
        ],
        compiler_params=pltpu.CompilerParams(
            collective_id=0, has_side_effects=True, vmem_limit_bytes=24 * 1024 * 1024
        ),
        name="to_spectral",
    )(
        *[
            pltpu.with_memory_space_constraint(value, pltpu.HBM)
            for value in (
                row_lengths,
                band_map,
                fold_map.T,
                band_map.reshape(1, LAT),
                grid.reshape(FIELDS, 2, WIDTH),
                jnp.transpose(legendre, (0, 2, 1)),
                to_modes,
                back_modes,
                mode_rates.reshape(1, ALL_FIELDS),
            )
        ]
    )
    held = [pltpu.with_memory_space_constraint(value, pltpu.VMEM) for value in held]
    spectral, grid_out = pl.pallas_call(
        points_kernel,
        out_shape=(
            jax.ShapeDtypeStruct(spec_shape, F32),
            jax.ShapeDtypeStruct((FIELDS, 2, WIDTH), BF16),
        ),
        in_specs=[vmem] * 7,
        out_specs=(anywhere, vmem),
        scratch_shapes=[pltpu.SMEM((8, 128), I32), pltpu.SemaphoreType.DMA((2,))],
        compiler_params=pltpu.CompilerParams(vmem_limit_bytes=24 * 1024 * 1024),
        name="to_points",
    )(*held)
    return jnp.transpose(spectral, (0, 2, 1, 3)), grid_out.reshape(FIELDS, 1, 2, WIDTH)


def solution(mesh):
    placed = (
        P("fld", "lat", None, None),
        P(),
        P(),
        P(),
        P(("lat", "fld"), None, None),
        P(),
        P(),
        P(),
    )
    return jax.shard_map(
        per_device,
        mesh=mesh,
        in_specs=placed,
        out_specs=(P(None, None, ("lat", "fld"), None), P("fld", "lat", None, None)),
        check_vma=False,
    )
```

```python
import math
import random

import jax
import jax.numpy as jnp
from jax import lax
from jax.experimental import pallas as pl
from jax.experimental.pallas import tpu as pltpu
from jax.sharding import PartitionSpec as P

HIGH = lax.Precision.HIGHEST
MESH = pl.DeviceIdType.MESH
F32, BF16, I32 = jnp.float32, jnp.bfloat16, jnp.int32
NT = (((1,), (1,)), ((), ()))
TN = (((0,), (0,)), ((), ()))

LAT, FLD = 32, 4
DEVS = LAT * FLD
FIELDS = 5
ALL_FIELDS = FIELDS * FLD
SLOTS = 10
PAIRS = SLOTS // 2
PLACES = 1281
CUT = 1279
WIDTH = 5248
WAVES = DEVS * SLOTS
HALF = 656
GROUP = 256
ROWS = 40
MAIN = PLACES - 1
UNROLL = 41
STEP = 16
BLOCKS = HALF // STEP
LANES = 1408
CHUNK = 512
CHUNKS = 11


def iota(shape, dim):
    return lax.broadcasted_iota(I32, shape, dim)


def dot(a, b, precision=None):
    return jnp.dot(a, b, precision=precision, preferred_element_type=F32)


def dot_tn(a, b):
    return lax.dot_general(a, b, TN, preferred_element_type=F32)


def dot_nt(a, b):
    return lax.dot_general(a, b, NT, preferred_element_type=F32)


SIN_TERMS = [(-1) ** k * math.pi ** (2 * k + 1) / math.factorial(2 * k + 1) for k in range(6)]
COS_TERMS = [(-1) ** k * math.pi ** (2 * k) / math.factorial(2 * k) for k in range(7)]


def horner(terms, square):
    total = jnp.full_like(square, terms[-1])
    for term in terms[-2::-1]:
        total = total * square + term
    return total


def turn(product, period, inverse):
    rest = product - period * jnp.round(product * inverse)
    part = rest * inverse
    square = part * part
    half_sin = part * horner(SIN_TERMS, square)
    half_cos = horner(COS_TERMS, square)
    return 1.0 - 2.0 * half_sin * half_sin, 2.0 * half_sin * half_cos


def row_of(value):
    return jnp.concatenate([value[s : s + 1] for s in range(SLOTS)], axis=1)


def split(value):
    upper = value.astype(BF16)
    return upper, (value - upper.astype(F32)).astype(BF16)


def triple(left):
    upper, lower = split(left)
    return jnp.concatenate([upper, upper, lower], axis=1)


def dot_triple(left, right):
    upper, lower = split(right)
    return dot(left, jnp.concatenate([upper, lower, upper], axis=0))


def offsets():
    hops = (0, 1, 2, 1)
    steps = [(x, y, z, c) for y in range(4) for z in range(4) for c in range(2) for x in range(4)][1:]
    random.Random(5).shuffle(steps)
    return sorted(steps, key=lambda step: -(hops[step[0]] + hops[step[1]] + hops[step[2]]))


def send_kernel(
    len_hbm, band_s_hbm, fold_hbm, band_hbm, grid_hbm, leg_hbm, to_hbm, back_hbm, rate_hbm,
    spec_ref, cos_tab, sin_tab, tre_ref, tim_ref, size_ref, sel_ref,
    len_ref, band_s_ref, fold_s_ref, fold_ref, band_ref, grid_ref, leg_ref, to_ref, back_ref, rate_ref,
    wc_ref, ws_ref, rev_ref, leg4_ref, inv_ref, damp_ref, acc_c, acc_s, turned,
    send1, recv1, send2, recv2, in_sems, sems,
):
    lat = lax.axis_index("lat")
    fld = lax.axis_index("fld")
    owner = lat * FLD + fld

    moves = [
        pltpu.make_async_copy(source, dest, in_sems.at[k])
        for k, (source, dest) in enumerate(
            (
                (len_hbm, len_ref), (band_s_hbm, band_s_ref), (fold_hbm, fold_ref), (grid_hbm, grid_ref),
                (fold_hbm, fold_s_ref), (band_hbm, band_ref), (to_hbm, to_ref), (back_hbm, back_ref),
                (rate_hbm, rate_ref), (leg_hbm, leg_ref),
            )
        )
    ]

    high, middle, core = lat // 8, lax.rem(lat // 2, 4), lax.rem(lat, 2)
    xs, ys, zs_, cs = (
        [at] + [lax.rem(at + k, size) for k in range(1, size)]
        for at, size in ((fld, 4), (high, 4), (middle, 4), (core, 2))
    )
    peers = [(ys[y] * 8 + zs_[z] * 2 + cs[c], xs[x]) for x, y, z, c in offsets()]

    barrier = pltpu.get_barrier_semaphore()
    for o_lat, o_fld in peers:
        pl.semaphore_signal(barrier, inc=1, device_id={"lat": o_lat, "fld": o_fld}, device_id_type=MESH)

    for move in moves:
        move.start()
    sel_ref[...] = selection(False)
    rev_ref[...] = selection(True)

    for move in moves[:4]:
        move.wait()
    length = len_ref[band_s_ref[lat]]
    waves = row_of(fold_ref[...].astype(F32))
    full = jnp.full((1, WAVES), length.astype(F32), F32)
    size_ref[...] = jnp.full((8, 128), length, I32)
    quarter = full * 0.25
    inv_quarter = 1.0 / quarter
    scale = 1.0 / jnp.sqrt(full)
    keep = jnp.where(waves * 2.0 < full, 1.0, 0.0)
    zc, zs = turn(waves, full, 1.0 / full)

    base_c, base_s = turn(iota((STEP, WAVES), 0).astype(F32) * waves, quarter, inv_quarter)
    for start in range(0, 48, 8):
        c, s = turn((iota((8, WAVES), 0) + start).astype(F32) * (waves * float(STEP)), quarter, inv_quarter)
        wc_ref[start : start + 8, :] = c
        ws_ref[start : start + 8, :] = s
    points = jnp.concatenate([grid_ref[f].astype(F32) for f in range(FIELDS)], axis=0)
    points = jnp.where(iota((2 * FIELDS, WIDTH), 1) < length, points, 0.0)
    points = jnp.concatenate([points, jnp.zeros((16 - 2 * FIELDS, WIDTH), F32)], axis=0).astype(BF16)
    points = jnp.concatenate([points, jnp.zeros((16, CHUNK * CHUNKS - WIDTH), BF16)], axis=1)
    points = jnp.concatenate([points[:, CHUNK * k : CHUNK * (k + 1)] for k in range(CHUNKS)], axis=0)

    def by_phase(values, order):
        return jnp.concatenate(
            [
                jnp.concatenate([values[16 * k : 16 * (k + 1), 128 * b : 128 * (b + 1)] for k in order], axis=1)
                for b in range(4)
            ],
            axis=0,
        )

    ahead = by_phase(dot(points, sel_ref[...]), range(6))[:, :HALF]
    behind = by_phase(dot(points, rev_ref[...]), range(CHUNKS - 1, -1, -1))
    behind = pltpu.roll(behind, length // 4 + 1, 1)[:, :HALF]
    twice = (iota((64, HALF), 1) * 8).astype(F32)
    whole = full[:, :HALF]
    share = jnp.where(twice < whole, 1.0, jnp.where(twice == whole, 0.5, 0.0))

    plus = ((ahead + behind) * share).astype(BF16)
    minus = ((ahead - behind) * share).astype(BF16)
    for start in range(0, WAVES, GROUP):
        lanes = slice(start, start + GROUP)
        bc, bs = base_c[:, lanes], base_s[:, lanes]

        def fill(j, carry):
            c, s = wc_ref[pl.ds(j, 1), lanes], ws_ref[pl.ds(j, 1), lanes]
            rows = pl.ds(pl.multiple_of(j * STEP, STEP), STEP)
            cos_tab[rows, lanes] = (bc * c - bs * s).astype(BF16)
            sin_tab[rows, lanes] = (bs * c + bc * s).astype(BF16)
            return carry

        lax.fori_loop(0, BLOCKS, fill, 0, unroll=UNROLL)
        acc_c[:, lanes] = dot(plus, cos_tab[:, lanes])
        acc_s[:, lanes] = dot(minus, sin_tab[:, lanes])
    re, im = acc_c[48:64, :], -acc_s[48:64, :]
    for b in (2, 1, 0):
        re, im = (
            re * zc + im * zs + acc_c[16 * b : 16 * (b + 1), :],
            im * zc - re * zs - acc_s[16 * b : 16 * (b + 1), :],
        )
    for c, part in enumerate((re, im)):
        part = part * (scale * keep)
        packed = jnp.concatenate(
            [part[0:10, 128 * s : 128 * (s + 1)] for s in range(SLOTS)] + [jnp.zeros((28, 128), F32)], axis=0
        )
        send1[:, c, :] = packed.T

    def exchange(source, dest, sem, row, row_at):
        for o_lat, o_fld in peers:
            pltpu.make_async_remote_copy(
                src_ref=source.at[row_at(o_lat, o_fld)],
                dst_ref=dest.at[row],
                send_sem=sems.at[sem],
                recv_sem=sems.at[sem + 1],
                device_id={"lat": o_lat, "fld": o_fld},
                device_id_type=MESH,
            ).start()
        dest[row] = source[row_at(lat, fld)]

    def finish(buffer, sem):
        some = buffer.at[pl.ds(0, DEVS - 1)]
        pltpu.make_async_copy(some, some, sems.at[sem]).wait()

    by_owner = lambda a, b: a * FLD + b
    by_group = lambda a, b: b * LAT + a
    pl.semaphore_wait(barrier, DEVS - 1)
    exchange(send1, recv1, 0, by_group(lat, fld), by_owner)

    for move in moves[4:]:
        move.wait()
    perm = jnp.where(iota((LAT, LAT), 0) == band_ref[...], 1.0, 0.0)
    rates = jnp.sum(
        jnp.where((iota((ROWS, ALL_FIELDS), 0) >> 1) == iota((ROWS, ALL_FIELDS), 1), rate_ref[...], 0.0),
        axis=1, keepdims=True,
    )
    place = iota((1, MAIN), 1)
    quad = iota((1, 128), 1) >> 5
    wide_perm = jnp.concatenate([perm] * 4, axis=1).astype(BF16)
    final = 1.0 / (1.0 + rates)
    edges = []
    inv_ref[ROWS * PAIRS :, :] = jnp.zeros((8, MAIN), F32)
    for p in range(PAIRS):
        first = fold_s_ref[2 * p, owner]
        value = dot_tn(perm.astype(BF16), leg_ref[p, :, 0:MAIN].astype(BF16))
        partner = place > CUT - first
        one = jnp.where(partner, 0.0, value)
        two = jnp.where(partner, value, 0.0)
        sign_one = jnp.where((place & 1) == 1, -1.0, 1.0)
        sign_two = jnp.where(((place + first) & 1) == 1, -1.0, 1.0)
        for k, masked in enumerate((one, one * sign_one, two, two * sign_two)):
            leg4_ref[128 * p + 32 * k : 128 * p + 32 * (k + 1), :] = masked.astype(BF16)
        degree = jnp.where(partner, place - 1, first + place).astype(F32)
        tau = degree * (degree + 1.0) * (1.0 / float(CUT * (CUT + 1)))
        inv_ref[ROWS * p : ROWS * (p + 1), :] = 1.0 / (1.0 + rates * tau)
        edge = dot_tn(leg_ref[p, :, MAIN:PLACES].astype(BF16), wide_perm)
        odd = ((iota((1, 128), 1) * 0 + MAIN + first) & 1) == 1
        edges.append(jnp.where(quad < 2, 0.0, jnp.where((quad == 3) & odd, -edge, edge)))

    rows, cols = iota((ROWS, 64), 0), iota((ROWS, 64), 1)
    pick = jnp.where((iota((ROWS, 20), 0) >> 1) == iota((ROWS, 20), 1), 1.0, 0.0)
    spread_col = iota((20, 64), 1)
    spread = jnp.where(
        ((spread_col & 7) < FIELDS) & (iota((20, 64), 0) == (spread_col >> 4) * FIELDS + (spread_col & 7)), 1.0, 0.0
    )
    to_all = dot(dot(pick, to_ref[...], HIGH), spread, HIGH)
    to_all = triple(jnp.where((rows & 1) == ((cols >> 3) & 1), to_all, 0.0))
    pick_t = jnp.where(iota((20, ROWS), 0) == (iota((20, ROWS), 1) >> 1), 1.0, 0.0)
    half = dot(back_ref[...], pick_t, HIGH)
    back_rows = dot(pick, half, HIGH)
    back_rows = jnp.where((iota((ROWS, ROWS), 0) & 1) == (iota((ROWS, ROWS), 1) & 1), back_rows, 0.0)
    blank = jnp.zeros((ROWS, ROWS), F32)
    back_pair = jnp.concatenate(
        [jnp.concatenate([back_rows, blank], axis=1), jnp.concatenate([blank, back_rows], axis=1)], axis=0
    )
    back_pair = jnp.concatenate(split(back_pair), axis=0)

    spread_row = iota((64, 20), 0)
    spread_t = jnp.where(
        ((spread_row & 7) < FIELDS) & (iota((64, 20), 1) == (spread_row >> 4) * FIELDS + (spread_row & 7)), 1.0, 0.0
    )
    back_all = dot(spread_t, half, HIGH)
    back_all = jnp.where(((iota((64, ROWS), 0) >> 3) & 1) == (iota((64, ROWS), 1) & 1), back_all, 0.0)
    back_all = triple(back_all)

    finish(recv1, 1)

    for c in range(2):
        turned[c] = recv1[:, c, :].T
    block = iota((16, 128), 1) >> 5
    gathered = []
    for p in range(PAIRS):
        rolled = []
        for j in range(4):
            at = 10 * (2 * p + (j >> 1)) + (j & 1)
            source = jnp.concatenate([turned[c, pl.ds(at, 8, stride=2), :] for c in range(2)], axis=0)
            rolled.append([source] + [pltpu.roll(source, 32 * k, 1) for k in range(1, 4)])
        parts = []
        for g in range(FLD):
            total = rolled[0][(0 - g) % 4]
            for j in range(1, 4):
                total = jnp.where(block == j, rolled[j][(j - g) % 4], total)
            parts.append(total)
        gathered.append(jnp.concatenate(parts, axis=0))
    modes_at = dot_triple(to_all, jnp.concatenate(gathered, axis=1))
    nothing = jnp.zeros((ROWS, 128), F32)
    sums, ends = [], []
    for p in range(0, PAIRS, 2):
        at = [modes_at[:, 128 * q : 128 * (q + 1)] if q < PAIRS else nothing for q in (p, p + 1)]
        both = jnp.concatenate(
            [jnp.concatenate([at[0], nothing], axis=1), jnp.concatenate([nothing, at[1]], axis=1)], axis=0
        ).astype(BF16)
        if p + 1 == PAIRS:
            both = both[0:48, 0:128]
        count = both.shape[0]
        tables = slice(128 * p, 128 * p + both.shape[1])
        places = inv_ref[ROWS * p : ROWS * p + count, :]
        damped = (dot(both, leg4_ref[tables, :]) * places).astype(BF16)
        damp_ref[p // 2, 0:count, :] = damped
        total = dot_nt(damped, leg4_ref[tables, :])
        for k in range(min(2, PAIRS - p)):
            exact = at[k].astype(BF16).astype(F32)
            end = jnp.sum(exact * edges[p + k], axis=1, keepdims=True) * final
            ends.append(end)
            sums.append(total[ROWS * k : ROWS * (k + 1), 128 * k : 128 * (k + 1)] + end * edges[p + k])

    returned = dot_triple(back_all, jnp.concatenate(sums, axis=1))
    turned[...] = jnp.zeros_like(turned)
    for p in range(PAIRS):
        rolled = []
        for g in range(FLD):
            source = returned[16 * g : 16 * (g + 1), 128 * p : 128 * (p + 1)]
            rolled.append([source] + [pltpu.roll(source, 32 * k, 1) for k in range(1, 4)])
        for j in range(4):
            total = rolled[0][(0 - j) % 4]
            for g in range(1, 4):
                total = jnp.where(block == g, rolled[g][(g - j) % 4], total)
            at = 10 * (2 * p + (j >> 1)) + (j & 1)
            for c in range(2):
                turned[c, pl.ds(at, 8, stride=2), :] = total[8 * c : 8 * (c + 1)]
    for c in range(2):
        send2[:, c, :] = turned[c].T
    exchange(send2, recv2, 2, by_owner(lat, fld), by_group)

    lane = iota((ROWS, 128), 1)
    last = jnp.zeros((ROWS, 128), F32)
    for p in range(PAIRS):
        last = jnp.where(lane == p, ends[p], last)
    last = dot(back_rows, last, HIGH)
    for p in range(0, PAIRS, 2):
        count = 2 if p + 1 < PAIRS else 1
        depth = 2 * ROWS if count == 2 else 48
        spec = dot(back_pair[:, 0:depth], damp_ref[p // 2, 0:depth, :])
        spec = spec[0 : 2 * ROWS] + spec[2 * ROWS : 4 * ROWS]
        for k in range(count):
            block_rows = jnp.concatenate(
                [spec[ROWS * k : ROWS * (k + 1)], last[:, p + k : p + k + 1]], axis=1
            )
            for g in range(ALL_FIELDS):
                spec_ref[g, p + k, :, :] = block_rows[2 * g : 2 * g + 2]

    finish(recv2, 3)

    for c in range(2):
        turned[c] = recv2[:, c, :].T
    weight = keep * jnp.where(waves == 0.0, 1.0, 2.0)
    re, im = (
        jnp.concatenate([turned[c, 10 * s : 10 * s + 16, :] for s in range(SLOTS)], axis=1) * weight for c in range(2)
    )
    for b in range(4):
        tre_ref[16 * b : 16 * (b + 1), :] = re.astype(BF16)
        tim_ref[16 * b : 16 * (b + 1), :] = im.astype(BF16)
        if b < 3:
            re, im = re * zc - im * zs, re * zs + im * zc
    finish(send1, 0)
    finish(send2, 2)


def points_kernel(
    spec_in, cos_tab, sin_tab, tre_ref, tim_ref, size_ref, sel_ref, spec_out, out_ref, size_smem, sems
):
    move = pltpu.make_async_copy(spec_in, spec_out, sems.at[0])
    move.start()
    size = pltpu.make_async_copy(size_ref, size_smem, sems.at[1])
    size.start()
    flip = jnp.where(iota((128, 128), 0) + iota((128, 128), 1) == 127, 1.0, 0.0).astype(BF16)
    even = dot_nt(tre_ref[...], cos_tab[...])
    odd = dot_nt(tim_ref[...], sin_tab[...])
    size.wait()
    length = size_smem[0, 0]
    scale = 1.0 / jnp.sqrt(jnp.full((1, HALF), length.astype(F32), F32))
    ahead = (even - odd) * scale
    behind = ((even + odd) * scale).astype(BF16)
    behind = jnp.concatenate([behind, jnp.zeros((64, 768 - HALF), BF16)], axis=1)
    behind = dot(jnp.concatenate([behind[:, 128 * k : 128 * (k + 1)] for k in range(6)], axis=0), flip)
    behind = jnp.concatenate(
        [jnp.zeros((64, LANES - 768), F32)] + [behind[64 * k : 64 * (k + 1)] for k in range(5, -1, -1)], axis=1
    )
    behind = pltpu.roll(behind, length // 4 + 1, 1)
    ahead = jnp.concatenate([ahead, jnp.zeros((64, LANES - HALF), F32)], axis=1)
    across = iota((64, LANES), 1)
    total = jnp.where(across * 8 <= length, ahead, jnp.where(across * 4 < length, behind, 0.0)).astype(BF16)
    total = jnp.concatenate(
        [
            jnp.concatenate([total[16 * b : 16 * (b + 1), 128 * k : 128 * (k + 1)] for b in range(4)], axis=1)
            for k in range(CHUNKS)
        ],
        axis=0,
    )
    total = dot_nt(total, sel_ref[...])
    total = jnp.concatenate([total[16 * k : 16 * (k + 1)] for k in range(CHUNKS)], axis=1)[:, :WIDTH]
    for f in range(FIELDS):
        out_ref[f, :, :] = total[2 * f : 2 * f + 2].astype(BF16)
    move.wait()


def selection(flipped):
    column = iota((1, CHUNK), 1)
    across = column & 127
    target = (127 - across if flipped else across) * 4 + (column >> 7)
    return jnp.where(iota((CHUNK, CHUNK), 0) == target, 1.0, 0.0).astype(BF16)


def per_device(grid, row_lengths, band_map, fold_map, legendre, to_modes, back_modes, mode_rates):
    vmem = pl.BlockSpec(memory_space=pltpu.VMEM)
    anywhere = pl.BlockSpec(memory_space=pl.ANY)
    spec_shape = (ALL_FIELDS, PAIRS, 2, PLACES)
    held = pl.pallas_call(
        send_kernel,
        out_shape=(
            pltpu.VMEM(spec_shape, F32),
            pltpu.VMEM((HALF, WAVES), BF16),
            pltpu.VMEM((HALF, WAVES), BF16),
            pltpu.VMEM((64, WAVES), BF16),
            pltpu.VMEM((64, WAVES), BF16),
            pltpu.VMEM((8, 128), I32),
            pltpu.VMEM((CHUNK, CHUNK), BF16),
        ),
        in_specs=[pl.BlockSpec(memory_space=pltpu.HBM)] * 9,
        out_specs=(vmem,) * 7,
        scratch_shapes=[
            pltpu.SMEM((LAT,), I32),
            pltpu.SMEM((LAT,), I32),
            pltpu.SMEM((SLOTS, DEVS), I32),
            pltpu.VMEM((SLOTS, DEVS), I32),
            pltpu.VMEM((1, LAT), I32),
            pltpu.VMEM((FIELDS, 2, WIDTH), BF16),
            pltpu.VMEM((PAIRS, LAT, PLACES), F32),
            pltpu.VMEM((ALL_FIELDS, ALL_FIELDS), F32),
            pltpu.VMEM((ALL_FIELDS, ALL_FIELDS), F32),
            pltpu.VMEM((1, ALL_FIELDS), F32),
            pltpu.VMEM((48, WAVES), F32),
            pltpu.VMEM((48, WAVES), F32),
            pltpu.VMEM((CHUNK, CHUNK), BF16),
            pltpu.VMEM((PAIRS * 128, MAIN), BF16),
            pltpu.VMEM((PAIRS * ROWS + 8, MAIN), F32),
            pltpu.VMEM(((PAIRS + 1) // 2, 2 * ROWS, MAIN), BF16),
            pltpu.VMEM((64, WAVES), F32),
            pltpu.VMEM((64, WAVES), F32),
            pltpu.VMEM((2, 128, 128), F32),
            pltpu.VMEM((DEVS, 2, 128), F32),
            pltpu.VMEM((DEVS, 2, 128), F32),
            pltpu.VMEM((DEVS, 2, 128), F32),
            pltpu.VMEM((DEVS, 2, 128), F32),
            pltpu.SemaphoreType.DMA((10,)),
            pltpu.SemaphoreType.DMA((4,)),
        ],
        compiler_params=pltpu.CompilerParams(
            collective_id=0, has_side_effects=True, vmem_limit_bytes=24 * 1024 * 1024
        ),
        name="to_spectral",
    )(
        *[
            pltpu.with_memory_space_constraint(value, pltpu.HBM)
            for value in (
                row_lengths,
                band_map,
                fold_map.T,
                band_map.reshape(1, LAT),
                grid.reshape(FIELDS, 2, WIDTH),
                jnp.transpose(legendre, (0, 2, 1)),
                to_modes,
                back_modes,
                mode_rates.reshape(1, ALL_FIELDS),
            )
        ]
    )
    held = [pltpu.with_memory_space_constraint(value, pltpu.VMEM) for value in held]
    spectral, grid_out = pl.pallas_call(
        points_kernel,
        out_shape=(
            jax.ShapeDtypeStruct(spec_shape, F32),
            jax.ShapeDtypeStruct((FIELDS, 2, WIDTH), BF16),
        ),
        in_specs=[vmem] * 7,
        out_specs=(anywhere, vmem),
        scratch_shapes=[pltpu.SMEM((8, 128), I32), pltpu.SemaphoreType.DMA((2,))],
        compiler_params=pltpu.CompilerParams(vmem_limit_bytes=24 * 1024 * 1024),
        name="to_points",
    )(*held)
    return jnp.transpose(spectral, (0, 2, 1, 3)), grid_out.reshape(FIELDS, 1, 2, WIDTH)


def solution(mesh):
    placed = (
        P("fld", "lat", None, None),
        P(),
        P(),
        P(),
        P(("lat", "fld"), None, None),
        P(),
        P(),
        P(),
    )
    return jax.shard_map(
        per_device,
        mesh=mesh,
        in_specs=placed,
        out_specs=(P(None, None, ("lat", "fld"), None), P("fld", "lat", None, None)),
        check_vma=False,
    )
```
